256 devices in a mesh: slab: 32 (over z, x_lo, core), angle: 8 (over x_hi, y).
Axes of the slice: x: 4 (x_hi: 2, x_lo: 2; x = x_hi * 2 + x_lo), y: 4, z: 8, core: 2. Of those that a mesh axis runs over, the one named last changes fastest.
Arguments:
- volume: bfloat16 [2, 32, 128, 2048], P(None, 'slab'), may hold values from -1 to 1
- consensus: bfloat16 [2, 32, 128, 2048], P(None, 'slab'), may hold values from -3 to 3
- probe: bfloat16 [2, 128, 128], replicated, may hold values from -4.1875 to 4.1875
- intensities: bfloat16 [8, 128, 512, 128], P('angle', None, 'slab'), may hold values from 0 to 4
- positions: int32 [8, 512], P('angle', 'slab'), may hold values from 0 to 1920
- offsets: int32 [8, 32], P('angle', 'slab'), may hold values from 0 to 2047
Outputs:
- updated: float32 [2, 32, 128, 2048], P(None, 'slab')
The draws below stay inside these ranges and needn't reach their ends.
All inputs are finite; a program needn't handle non-finite values.
Results may differ from the reference program's by a relative error of at most 0.0085.
Values may be sent and summed in bfloat16 or wider, within the bound.
A program may use at most 64 MiB of HBM per device.

```python
import math
import jax
import jax.numpy as jnp
from jax import lax

NX = 2048
PW = 128
NZ = 32
ANGLES = 8
P_SIZE = 512


def with_ends(values, stream_key, least, top_value):
    longest = values.shape.index(max(values.shape))
    spots = []
    for shift in (0, 1):
        where = [jax.random.randint(jax.random.fold_in(stream_key, axis), (), 0, length) for axis, length in enumerate(values.shape)]
        where[longest] = (where[longest] + shift) % values.shape[longest]
        spots.append(tuple(where))
    return values.at[spots[0]].set(least).at[spots[1]].set(top_value)


def steps_of(key, shape, shards, smallest, top_value):
    gain = 1.0
    for position, shards_of in shards:
        steps = jax.random.uniform(jax.random.fold_in(jax.random.fold_in(key, 6), position), (shards_of,), jnp.float32, smallest / len(shards), top_value / len(shards))
        gain = gain * jnp.repeat(jnp.exp(steps), shape[position] // shards_of).reshape((-1,) + (1,) * (len(shape) - 1 - position))
    return gain


def scatter_about(key, dims, deviation, bound, split=(), kind=jnp.bfloat16):
    values = deviation * jax.random.normal(key, dims, jnp.float32)
    if split:
        values = values * steps_of(key, dims, split, -0.22, 0.18)
    return jnp.clip(values, -bound, bound).astype(kind)


def setup_inputs(seed: int = 0) -> dict:
    keys = jax.random.split(jax.random.key(seed), 7)
    return {
        "volume": scatter_about(keys[0], (2, NZ, PW, NX), NZ ** -0.5, 1.0, ((1, 32),)),
        "consensus": scatter_about(keys[1], (2, NZ, PW, NX), 0.5, 3.0, ((1, 32),)),
        "probe": scatter_about(keys[2], (2, PW, PW), 0.7, 4.1875),
        "intensities": jnp.clip(4.0 * jax.random.uniform(keys[3], (ANGLES, PW, P_SIZE, PW), jnp.float32) ** steps_of(keys[3], (ANGLES, PW, P_SIZE, PW), ((0, 8), (2, 32)), -0.2, 0.2), 0.0, 4.0).astype(jnp.bfloat16),
        "positions": with_ends(jax.random.randint(keys[4], (ANGLES, P_SIZE), 0, NX - PW + 1), jax.random.fold_in(keys[4], 1), 0, NX - PW).astype(jnp.int32),
        "offsets": with_ends(jax.random.randint(keys[5], (ANGLES, NZ), 0, NX), jax.random.fold_in(keys[5], 1), 0, NX - 1).astype(jnp.int32),
    }


mix_weight = 0.5

def dft_tables(length):
    indices = jnp.arange(length, dtype=jnp.int32)
    phases = (indices[:, None] * indices[None, :] % length).astype(jnp.float32) * (2.0 * math.pi / length)
    factor = 1.0 / math.sqrt(length)
    real_t = (jnp.cos(phases) * factor).astype(jnp.bfloat16)
    imag_t = (-jnp.sin(phases) * factor).astype(jnp.bfloat16)
    right_fwd = jnp.concatenate([jnp.concatenate([real_t, imag_t], axis=1), jnp.concatenate([-imag_t, real_t], axis=1)], axis=0)
    right_inv = jnp.concatenate([jnp.concatenate([real_t, -imag_t], axis=1), jnp.concatenate([imag_t, real_t], axis=1)], axis=0)
    return (real_t, imag_t, right_fwd, right_inv)

def wave_grad(patch, probe, measured, tables):
    real_t, imag_t, right_fwd, right_inv = tables
    width = probe.shape[-1]
    probe_re = probe[0].astype(jnp.float32)[:, None, :]
    probe_im = probe[1].astype(jnp.float32)[:, None, :]
    patch_re = patch[0].astype(jnp.float32)
    patch_im = patch[1].astype(jnp.float32)
    exit_wave = jnp.concatenate([probe_re * patch_re - probe_im * patch_im, probe_re * patch_im + probe_im * patch_re], axis=-1).astype(jnp.bfloat16)
    half = jnp.einsum('jbk,kc->jbc', exit_wave.astype(jnp.float32), right_fwd.astype(jnp.float32)).astype(jnp.bfloat16)
    first = jnp.einsum('ij,jbc->ibc', real_t.astype(jnp.float32), half.astype(jnp.float32))
    second = jnp.einsum('ij,jbc->ibc', imag_t.astype(jnp.float32), half.astype(jnp.float32))
    far_re = first[..., :width] - second[..., width:]
    far_im = first[..., width:] + second[..., :width]
    misfit = far_re * far_re + far_im * far_im - measured.astype(jnp.float32)
    residual_wave = jnp.concatenate([misfit * far_re, misfit * far_im], axis=-1).astype(jnp.bfloat16)
    back_half = jnp.einsum('jbk,kc->jbc', residual_wave.astype(jnp.float32), right_inv.astype(jnp.float32)).astype(jnp.bfloat16)
    first = jnp.einsum('ij,jbc->ibc', real_t.astype(jnp.float32), back_half.astype(jnp.float32))
    second = jnp.einsum('ij,jbc->ibc', imag_t.astype(jnp.float32), back_half.astype(jnp.float32))
    grad_re = first[..., :width] + second[..., width:]
    grad_im = first[..., width:] - second[..., :width]
    return jnp.stack([probe_re * grad_re + probe_im * grad_im, probe_re * grad_im - probe_im * grad_re])

def reference(volume, consensus, probe, intensities, positions, offsets):
    tables = dft_tables(PW)
    depth_ids = jnp.arange(NZ, dtype=jnp.int32)

    def project(offset_row):

        def add_depth(total, depth):
            slab_now = lax.dynamic_index_in_dim(volume, depth, 1, keepdims=False).astype(jnp.float32)
            shift_now = lax.dynamic_index_in_dim(offset_row, depth, 0, keepdims=False)
            return (total + jnp.roll(slab_now, -shift_now, axis=-1), None)
        total, _ = lax.scan(add_depth, jnp.zeros((2, PW, NX), jnp.float32), depth_ids)
        return total.astype(jnp.bfloat16)
    projection = lax.map(project, offsets)
    group = math.gcd(P_SIZE, 256)
    columns_base = jnp.arange(PW, dtype=jnp.int32)

    def angle_grad(items):
        proj_now, pos_row, measured_all = items
        pos_blocks = pos_row.reshape(P_SIZE // group, group)
        block_ids = jnp.arange(P_SIZE // group, dtype=jnp.int32)

        def add_block(total, item):
            block_pos, block_id = item
            cols = block_pos[:, None] + columns_base[None, :]
            patch = proj_now[:, :, cols]
            measured = lax.dynamic_slice_in_dim(measured_all, block_id * group, group, 1)
            grads = wave_grad(patch, probe, measured, tables)
            return (total.at[:, :, cols].add(grads), None)
        total, _ = lax.scan(add_block, jnp.zeros((2, PW, NX), jnp.float32), (pos_blocks, block_ids))
        return total
    detector_grad = lax.map(angle_grad, (projection, positions, intensities))
    angle_ids = jnp.arange(ANGLES, dtype=jnp.int32)

    def back_project(depth):

        def add_angle(total, angle_id):
            grad_now = lax.dynamic_index_in_dim(detector_grad, angle_id, 0, keepdims=False)
            shift_now = offsets[angle_id, depth]
            return (total + jnp.roll(grad_now, shift_now, axis=-1), None)
        total, _ = lax.scan(add_angle, jnp.zeros((2, PW, NX), jnp.float32), angle_ids)
        return total
    volume_grad = jnp.moveaxis(lax.map(back_project, depth_ids), 0, 1)
    rate = math.sqrt(NX / (P_SIZE * ANGLES * PW))
    current = volume.astype(jnp.float32)
    result = current - rate * volume_grad - mix_weight * (current - consensus.astype(jnp.float32))
    return result.astype(jnp.float32)
```

```python
import math

import jax
import jax.numpy as jnp
import ml_dtypes
import numpy as np
from jax import lax
from jax.experimental import pallas as pl
from jax.experimental.pallas import tpu as pltpu
from jax.sharding import PartitionSpec as P

MIX = 0.5
NX = 2048
PW = 128
LANES = 128
TILES = NX // LANES
NZC = 8
NXL = 2
NXH = 2
NY = 4
ANGLES = NXH * NY
BLOCK = 16
HALF = NX // 2
CHUNK = NX // NY
FAR_FIRST = (4, 3, 5, 2, 6, 1, 7, 0)
VMEM = 48 * 1024 * 1024


def dft_tables():
    indices = np.arange(PW, dtype=np.int64)
    phases = (indices[:, None] * indices[None, :] % PW).astype(np.float64) * (2.0 * math.pi / PW)
    factor = 1.0 / math.sqrt(PW)
    re = (np.cos(phases) * factor).astype(ml_dtypes.bfloat16)
    im = (-np.sin(phases) * factor).astype(ml_dtypes.bfloat16)
    forward = np.block([[re, im], [-im, re]])
    inverse = np.block([[re, -im], [im, re]])
    return forward.astype(ml_dtypes.bfloat16), inverse.astype(ml_dtypes.bfloat16)


class Here:
    def __init__(self):
        s = lax.axis_index("slab")
        a = lax.axis_index("angle")
        self.a = a
        self.c = lax.rem(s, 2)
        self.xl = lax.rem(lax.div(s, 2), 2)
        self.zc = lax.div(s, 4)
        self.y = lax.rem(a, NY)
        self.xh = lax.div(a, NY)
        self.m = self.xl * NZC + self.zc

    def z_of(self, rel):
        return lax.rem(self.zc + rel, NZC)

    def y_of(self, rel):
        return lax.rem(self.y + rel, NY)

    def x_of(self, flip):
        return 1 - self.xl if flip else self.xl

    def chip(self, rel_z, flip_x):
        return self.device(zc=self.z_of(rel_z), xl=self.x_of(flip_x))

    def angle_peer(self, flip_xh, rel_y):
        return self.device(xh=1 - self.xh if flip_xh else self.xh, y=self.y_of(rel_y))

    def device(self, zc=None, xl=None, c=None, xh=None, y=None):
        zc = self.zc if zc is None else zc
        xl = self.xl if xl is None else xl
        c = self.c if c is None else c
        xh = self.xh if xh is None else xh
        y = self.y if y is None else y
        return {"slab": zc * 4 + xl * 2 + c, "angle": xh * NY + y}

    @property
    def sibling(self):
        return self.device(c=1 - self.c)

    def greet(self):
        peers = [self.sibling]
        peers += [self.chip(r, f) for f in (0, 1) for r in range(NZC) if r or f]
        peers += [self.angle_peer(f, r) for f in (0, 1) for r in range(NY) if r or f]
        barrier = pltpu.get_barrier_semaphore()
        for peer in peers:
            pl.semaphore_signal(barrier, 1, device_id=peer, device_id_type=pl.DeviceIdType.MESH)
        pl.semaphore_wait(barrier, len(peers))


def rows16(block):
    return pl.ds(pl.multiple_of(block * BLOCK, BLOCK), BLOCK)


def half_cols(core):
    return pl.ds(pl.multiple_of(core * HALF, HALF), HALF)


def chunk_cols(y):
    return pl.ds(pl.multiple_of(y * CHUNK, CHUNK), CHUNK)


def remote(src, dst, send, recv, to):
    return pltpu.make_async_remote_copy(
        src_ref=src,
        dst_ref=dst,
        send_sem=send,
        recv_sem=recv,
        device_id=to,
        device_id_type=pl.DeviceIdType.MESH,
    )


def shifted_tiles(load, start, count):
    x = load(slice(None)).astype(jnp.float32)
    x = pltpu.roll(x, lax.rem(NX - start, NX), 1)
    return [x[:, j * LANES : (j + 1) * LANES] for j in range(count)]


def ring_quarters(here, piece, arrived, sems, order):
    s_up, s_dn, s_on, r_dn, r_up, r_on = sems
    up = here.angle_peer(0, 1)
    dn = here.angle_peer(0, NY - 1)
    y, y_dn, y_up, y_far = here.y, here.y_of(NY - 1), here.y_of(1), here.y_of(2)
    sent = []

    def start(src, dst, send, recv, to):
        copy = remote(src, dst, send, recv, to)
        copy.start()
        sent.append(copy)

    def onward(k):
        rel = order[k]
        if k % 2 == 0:
            remote(piece(rel, y_dn), piece(rel, y_dn), s_on.at[rel], r_dn.at[rel], up).wait_recv()
            start(piece(rel, y_dn), piece(rel, y_dn), s_on.at[rel], r_on.at[rel], up)
        else:
            remote(piece(rel, y_up), piece(rel, y_up), s_on.at[rel], r_up.at[rel], dn).wait_recv()
            start(piece(rel, y_up), piece(rel, y_up), s_on.at[rel], r_on.at[rel], dn)

    for k, rel in enumerate(order):
        arrived(rel)
        start(piece(rel, y), piece(rel, y), s_up.at[rel], r_dn.at[rel], up)
        start(piece(rel, y), piece(rel, y), s_dn.at[rel], r_up.at[rel], dn)
        if k >= 1:
            onward(k - 1)
    onward(len(order) - 1)

    def finish(k):
        rel = order[k]
        if k % 2 == 0:
            remote(piece(rel, y_up), piece(rel, y_up), s_on.at[rel], r_up.at[rel], dn).wait_recv()
        else:
            remote(piece(rel, y_dn), piece(rel, y_dn), s_on.at[rel], r_dn.at[rel], up).wait_recv()
        remote(piece(rel, y_far), piece(rel, y_far), s_on.at[rel], r_on.at[rel], up).wait_recv()

    return finish, sent


def project_kernel(
    vol, off, proj, offs_out, gath, acc, sib, offt, offv, offs_s,
    s_off, r_off, s_t1, r_t1, s_up, s_dn, s_on, r_dn, r_up, r_on,
    s_sib, r_sib, s_z, r_z, s_x, r_x, s_c, r_c, s_oa, r_oa, l_sem,
):
    here = Here()
    here.greet()
    sent = []

    def start(src, dst, send, recv, to):
        copy = remote(src, dst, send, recv, to)
        copy.start()
        sent.append(copy)

    cols = chunk_cols(here.y)
    for r in FAR_FIRST:
        for f in (0, 1):
            if not (r or f):
                continue
            slot = (NZC - r) % NZC
            to = here.chip(r, f)
            start(off, offt.at[here.m], s_off.at[f, r], r_off.at[f, slot], to)
            block = here.x_of(f) * NZC + here.z_of(r)
            start(vol.at[rows16(block), cols], gath.at[f, slot, :, cols], s_t1.at[f, r], r_t1.at[f, slot], to)
    offt[here.m] = off[...]
    gath[0, 0] = vol[rows16(here.m), :]
    acc[...] = jnp.zeros_like(acc)

    def piece(rel, y):
        if rel == 0:
            return gath.at[1, 0, :, chunk_cols(y)]
        return gath.at[:, rel, :, chunk_cols(y)]

    def arrived(rel):
        for f in (0, 1):
            if rel or f:
                part = gath.at[f, rel, :, cols]
                remote(part, part, s_t1.at[f, rel], r_t1.at[f, rel], here.chip(rel, f)).wait_recv()

    order = tuple((NZC - r) % NZC for r in FAR_FIRST)
    finish, ring_sent = ring_quarters(here, piece, arrived, (s_up, s_dn, s_on, r_dn, r_up, r_on), order)
    sent += ring_sent

    for f in (0, 1):
        for r in range(NZC):
            if r or f:
                part = offt.at[here.x_of(f) * NZC + here.z_of(r)]
                remote(part, part, s_off.at[f, r], r_off.at[f, r], here.chip(r, f)).wait_recv()
    for g in range(NXL * NZC):
        offv[g : g + 1, :] = offt[g, 0:1, :]
    for f in (0, 1):
        for r in range(NY):
            if r or f:
                back = (NY - r) % NY
                start(offv, offs_out.at[here.a], s_oa.at[f, r], r_oa.at[f, back], here.angle_peer(f, r))
    offs_out[here.a] = offv[...]
    down = pltpu.make_async_copy(offv, offs_s, l_sem)
    down.start()
    down.wait()

    for k in range(NZC):
        finish(k)

    def add_slot(i, carry):
        f = lax.div(i, NZC)
        rel = lax.rem(i, NZC)
        g = lax.rem(here.xl + f, NXL) * NZC + here.z_of(rel)
        tiles = shifted_tiles(lambda where: gath[f, rel, :, where], offs_s[g, 0], TILES)
        for j, tile in enumerate(tiles):
            acc[:, j * LANES : (j + 1) * LANES] += tile
        return carry

    lax.fori_loop(0, NXL * NZC, add_slot, 0)

    mine, other = half_cols(here.c), half_cols(1 - here.c)
    start(acc.at[:, other], sib, s_sib, r_sib, here.sibling)
    remote(sib, sib, s_sib, r_sib, here.sibling).wait_recv()
    proj[rows16(here.m), mine] = (acc[:, mine] + sib[...]).astype(jnp.bfloat16)

    own = proj.at[rows16(here.m), mine]
    for r in FAR_FIRST[:-1]:
        start(own, own, s_z.at[r], r_z.at[(NZC - r) % NZC], here.chip(r, 0))
    start(own, own, s_x.at[0], r_x.at[0], here.chip(0, 1))
    start(own, own, s_c.at[0, 0], r_c.at[0, 0], here.sibling)
    for rel in (1, 7, 2, 6, 3, 5, 4):
        got = proj.at[rows16(here.xl * NZC + here.z_of(rel)), mine]
        remote(got, got, s_z.at[rel], r_z.at[rel], here.chip(rel, 0)).wait_recv()
        start(got, got, s_x.at[rel], r_x.at[rel], here.chip(0, 1))
        start(got, got, s_c.at[0, rel], r_c.at[0, rel], here.sibling)
    for rel in (0, 1, 7, 2, 6, 3, 5, 4):
        got = proj.at[rows16(here.x_of(1) * NZC + here.z_of(rel)), mine]
        remote(got, got, s_x.at[rel], r_x.at[rel], here.chip(0, 1)).wait_recv()
        start(got, got, s_c.at[1, rel], r_c.at[1, rel], here.sibling)
    for f in (0, 1):
        for rel in (0, 1, 7, 2, 6, 3, 5, 4):
            got = proj.at[rows16(here.x_of(f) * NZC + here.z_of(rel)), other]
            remote(got, got, s_c.at[f, rel], r_c.at[f, rel], here.sibling).wait_recv()
    for f in (0, 1):
        for r in range(NY):
            if r or f:
                a_from = (1 - here.xh if f else here.xh) * NY + here.y_of(r)
                part = offs_out.at[a_from]
                remote(part, part, s_oa.at[f, r], r_oa.at[f, r], here.angle_peer(f, r)).wait_recv()
    for copy in sent:
        copy.wait_send()


def wave_kernel(proj, probe, measured, pos, forward, inverse, out, total):
    total[...] = jnp.zeros_like(total)
    pairs = measured.shape[1] // (2 * PW)

    def one_pair(pair, carry):
        p_re = probe[0].astype(jnp.float32)
        p_im = probe[1].astype(jnp.float32)
        fwd = forward[...]
        inv = inverse[...]
        starts = []
        exits = []
        for k in range(2):
            at = pos[2 * pair + k]
            first = jnp.minimum(lax.div(at, LANES), TILES - 2)
            inner = at - first * LANES
            where = pl.ds(pl.multiple_of(first * LANES, LANES), 2 * LANES)
            starts.append((where, inner))
            row = lax.broadcasted_iota(jnp.int32, (2 * LANES, PW), 0)
            col = lax.broadcasted_iota(jnp.int32, (2 * LANES, PW), 1)
            pick = jnp.where(row == col + inner, 1.0, 0.0).astype(jnp.bfloat16)
            patch = jnp.dot(proj[:, where], pick, preferred_element_type=jnp.float32)
            re, im = patch[:PW], patch[PW:]
            exits.append(
                jnp.concatenate([p_re * re - p_im * im, p_re * im + p_im * re], axis=1).astype(jnp.bfloat16)
            )
        half = jnp.dot(jnp.concatenate(exits, axis=0), fwd, preferred_element_type=jnp.float32).astype(jnp.bfloat16)
        half = jnp.concatenate(
            [
                jnp.concatenate([half[:PW, :PW], half[PW:, :PW]], axis=1),
                jnp.concatenate([half[:PW, PW:], half[PW:, PW:]], axis=1),
            ],
            axis=0,
        )
        far = jnp.dot(inv, half, preferred_element_type=jnp.float32)
        f_re, f_im = far[:PW], far[PW:]
        target = measured[:, pl.ds(pl.multiple_of(pair * 2 * PW, 2 * PW), 2 * PW)].astype(jnp.float32)
        misfit = f_re * f_re + f_im * f_im - target
        w_re = (misfit * f_re).astype(jnp.bfloat16)
        w_im = (misfit * f_im).astype(jnp.bfloat16)
        wave = jnp.concatenate(
            [
                jnp.concatenate([w_re[:, :PW], w_im[:, :PW]], axis=1),
                jnp.concatenate([w_re[:, PW:], w_im[:, PW:]], axis=1),
            ],
            axis=0,
        )
        back = jnp.dot(wave, inv, preferred_element_type=jnp.float32).astype(jnp.bfloat16)
        back = jnp.concatenate(
            [
                jnp.concatenate([back[:PW, :PW], back[PW:, :PW]], axis=1),
                jnp.concatenate([back[:PW, PW:], back[PW:, PW:]], axis=1),
            ],
            axis=0,
        )
        grad = jnp.dot(fwd, back, preferred_element_type=jnp.float32)
        for k, (where, inner) in enumerate(starts):
            g_re = grad[:PW, k * PW : (k + 1) * PW]
            g_im = grad[PW:, k * PW : (k + 1) * PW]
            patch_grad = jnp.concatenate(
                [p_re * g_re + p_im * g_im, p_re * g_im - p_im * g_re], axis=0
            ).astype(jnp.bfloat16)
            row = lax.broadcasted_iota(jnp.int32, (PW, 2 * LANES), 0)
            col = lax.broadcasted_iota(jnp.int32, (PW, 2 * LANES), 1)
            put = jnp.where(col == row + inner, 1.0, 0.0).astype(jnp.bfloat16)
            total[:, where] += jnp.dot(patch_grad, put, preferred_element_type=jnp.float32)
        return carry

    lax.fori_loop(0, pairs, one_pair, 0)
    out[...] = total[...].astype(jnp.bfloat16)


def volume_kernel(
    part, offs, out, cbuf, xsend, xbuf, zsend, zbuf, dgall, vsend,
    s_c, r_c, s_x, r_x, s_z, r_z, s_a, r_a, s_s, r_s,
    s_v, r_v, s_up, s_dn, s_on, r_dn, r_up, r_on,
):
    here = Here()
    here.greet()
    sent = []

    def start(src, dst, send, recv, to):
        copy = remote(src, dst, send, recv, to)
        copy.start()
        sent.append(copy)

    mine, other = half_cols(here.c), half_cols(1 - here.c)
    for f in (1, 0):
        for r in FAR_FIRST:
            src = part.at[rows16(here.x_of(f) * NZC + here.z_of(r)), other]
            start(src, cbuf.at[f, r], s_c.at[f, r], r_c.at[f, r], here.sibling)
    for r in FAR_FIRST:
        got = cbuf.at[1, r]
        remote(got, got, s_c.at[1, r], r_c.at[1, r], here.sibling).wait_recv()
        own = part[rows16(here.x_of(1) * NZC + here.z_of(r)), mine]
        xsend[r] = (own.astype(jnp.float32) + got[...].astype(jnp.float32)).astype(jnp.bfloat16)
        start(xsend.at[r], xbuf.at[r], s_x.at[r], r_x.at[r], here.chip(0, 1))
    total = None
    for r in FAR_FIRST:
        got = cbuf.at[0, r]
        remote(got, got, s_c.at[0, r], r_c.at[0, r], here.sibling).wait_recv()
        remote(xbuf.at[r], xbuf.at[r], s_x.at[r], r_x.at[r], here.chip(0, 1)).wait_recv()
        own = part[rows16(here.xl * NZC + here.z_of(r)), mine]
        value = own.astype(jnp.float32) + got[...].astype(jnp.float32) + xbuf[r].astype(jnp.float32)
        if r:
            zsend[r] = value.astype(jnp.bfloat16)
            slot = (NZC - r) % NZC
            start(zsend.at[r], zbuf.at[slot], s_z.at[r], r_z.at[slot], here.chip(r, 0))
        else:
            total = value
    for r in range(1, NZC):
        remote(zbuf.at[r], zbuf.at[r], s_z.at[r], r_z.at[r], here.chip(r, 0)).wait_recv()
        total = total + zbuf[r].astype(jnp.float32)
    dgall[here.a, :, mine] = total.astype(jnp.bfloat16)
    own = dgall.at[here.a, :, mine]
    peers = [(0, 2), (1, 2), (1, 1), (1, 3), (0, 1), (0, 3), (1, 0)]
    for f, r in peers:
        start(own, own, s_a.at[f, r], r_a.at[f, (NY - r) % NY], here.angle_peer(f, r))
    start(own, own, s_s.at[0, 0], r_s.at[0, 0], here.sibling)

    def angle_of(f, r):
        return (1 - here.xh if f else here.xh) * NY + here.y_of(r)

    for f, r in reversed(peers):
        got = dgall.at[angle_of(f, r), :, mine]
        remote(got, got, s_a.at[f, r], r_a.at[f, r], here.angle_peer(f, r)).wait_recv()
        start(got, got, s_s.at[f, r], r_s.at[f, r], here.sibling)
    for f, r in [(0, 0)] + peers:
        got = dgall.at[angle_of(f, r), :, other]
        remote(got, got, s_s.at[f, r], r_s.at[f, r], here.sibling).wait_recv()

    cols = chunk_cols(here.y)

    def gradient(f, r):
        g = here.x_of(f) * NZC + here.z_of(r)
        sums = [jnp.zeros((BLOCK, LANES), jnp.float32)] * (CHUNK // LANES)

        def add_angle(b, sums):
            first = lax.rem(here.y * CHUNK + NX - offs[b * NXL * NZC + g, 0], NX)
            tiles = shifted_tiles(lambda where: dgall[b, :, where], first, CHUNK // LANES)
            return [x + t for x, t in zip(sums, tiles)]

        sums = lax.fori_loop(0, ANGLES, add_angle, sums)
        return jnp.concatenate(sums, axis=1).astype(jnp.bfloat16)

    for r in FAR_FIRST:
        for f in (0, 1):
            value = gradient(f, r)
            if r or f:
                slot = (NZC - r) % NZC
                vsend[f, r] = value
                start(
                    vsend.at[f, r],
                    out.at[here.xl, rows16(here.zc), cols],
                    s_v.at[f, r],
                    r_v.at[f, slot],
                    here.chip(r, f),
                )
            else:
                out[here.xl, rows16(here.zc), cols] = value

    def piece(rel, y):
        return out.at[:, rows16(here.z_of(rel)), chunk_cols(y)]

    def arrived(rel):
        for f in (0, 1):
            if rel or f:
                got = out.at[here.x_of(f), rows16(here.z_of(rel)), cols]
                remote(got, got, s_v.at[f, rel], r_v.at[f, rel], here.chip(rel, f)).wait_recv()

    order = tuple((NZC - r) % NZC for r in FAR_FIRST)
    finish, ring_sent = ring_quarters(here, piece, arrived, (s_up, s_dn, s_on, r_dn, r_up, r_on), order)
    sent += ring_sent
    for k in range(NZC):
        finish(k)
    for copy in sent:
        copy.wait_send()


def dma(*shape):
    return pltpu.SemaphoreType.DMA(shape)


def vmem():
    return pl.BlockSpec(memory_space=pltpu.VMEM)


def smem():
    return pl.BlockSpec(memory_space=pltpu.SMEM)


def project(lines, off):
    return pl.pallas_call(
        project_kernel,
        out_shape=(
            jax.ShapeDtypeStruct((2 * PW, NX), jnp.bfloat16),
            jax.ShapeDtypeStruct((ANGLES, NXL * NZC, LANES), jnp.int32),
        ),
        in_specs=[vmem(), vmem()],
        out_specs=(vmem(), vmem()),
        scratch_shapes=[
            pltpu.VMEM((NXL, NZC, BLOCK, NX), jnp.bfloat16),
            pltpu.VMEM((BLOCK, NX), jnp.float32),
            pltpu.VMEM((BLOCK, HALF), jnp.float32),
            pltpu.VMEM((NXL * NZC, 8, LANES), jnp.int32),
            pltpu.VMEM((NXL * NZC, LANES), jnp.int32),
            pltpu.SMEM((NXL * NZC, LANES), jnp.int32),
            dma(NXL, NZC), dma(NXL, NZC), dma(NXL, NZC), dma(NXL, NZC),
            dma(NZC), dma(NZC), dma(NZC), dma(NZC), dma(NZC), dma(NZC),
            pltpu.SemaphoreType.DMA, pltpu.SemaphoreType.DMA,
            dma(NZC), dma(NZC), dma(NZC), dma(NZC),
            dma(NXL, NZC), dma(NXL, NZC),
            dma(NXH, NY), dma(NXH, NY),
            pltpu.SemaphoreType.DMA,
        ],
        compiler_params=pltpu.CompilerParams(collective_id=0, has_side_effects=True, vmem_limit_bytes=VMEM),
        name="project",
    )(lines, off)


def waves(proj, probe, measured, pos, forward, inverse):
    return pl.pallas_call(
        wave_kernel,
        out_shape=jax.ShapeDtypeStruct((2 * PW, NX), jnp.bfloat16),
        in_specs=[vmem(), vmem(), vmem(), smem(), vmem(), vmem()],
        out_specs=vmem(),
        scratch_shapes=[pltpu.VMEM((2 * PW, NX), jnp.float32)],
        compiler_params=pltpu.CompilerParams(vmem_limit_bytes=VMEM),
        name="waves",
    )(proj, probe, measured, pos, forward, inverse)


def volume_gradient(part, offs):
    bf16 = jnp.bfloat16
    return pl.pallas_call(
        volume_kernel,
        out_shape=jax.ShapeDtypeStruct((2, PW, NX), bf16),
        in_specs=[vmem(), smem()],
        out_specs=vmem(),
        scratch_shapes=[
            pltpu.VMEM((NXL, NZC, BLOCK, HALF), bf16),
            pltpu.VMEM((NZC, BLOCK, HALF), bf16),
            pltpu.VMEM((NZC, BLOCK, HALF), bf16),
            pltpu.VMEM((NZC, BLOCK, HALF), bf16),
            pltpu.VMEM((NZC, BLOCK, HALF), bf16),
            pltpu.VMEM((ANGLES, BLOCK, NX), bf16),
            pltpu.VMEM((NXL, NZC, BLOCK, CHUNK), bf16),
            dma(NXL, NZC), dma(NXL, NZC),
            dma(NZC), dma(NZC), dma(NZC), dma(NZC),
            dma(NXH, NY), dma(NXH, NY), dma(NXH, NY), dma(NXH, NY),
            dma(NXL, NZC), dma(NXL, NZC),
            dma(NZC), dma(NZC), dma(NZC), dma(NZC), dma(NZC), dma(NZC),
        ],
        compiler_params=pltpu.CompilerParams(collective_id=1, has_side_effects=True, vmem_limit_bytes=VMEM),
        name="volume_gradient",
    )(part, offs)


def per_device(volume, consensus, probe, intensities, positions, offsets):
    pos_count = positions.shape[1]
    forward, inverse = dft_tables()
    lines = volume.reshape(2 * PW, NX)
    off = jnp.broadcast_to(offsets, (8, LANES))
    measured = intensities.reshape(PW, pos_count * PW)
    proj, offs = project(lines, off)
    part = waves(proj, probe, measured, positions.reshape(-1), jnp.asarray(forward), jnp.asarray(inverse))
    grad = volume_gradient(part, offs.reshape(ANGLES * NXL * NZC, LANES))
    rate = math.sqrt(NX / (pos_count * lax.axis_size("slab") * ANGLES * PW))
    current = volume.astype(jnp.float32)
    step = grad[:, None].astype(jnp.float32)
    return current - rate * step - MIX * (current - consensus.astype(jnp.float32))


def solution(mesh):
    return jax.shard_map(
        per_device,
        mesh=mesh,
        in_specs=(
            P(None, "slab", None, None),
            P(None, "slab", None, None),
            P(),
            P("angle", None, "slab", None),
            P("angle", "slab"),
            P("angle", "slab"),
        ),
        out_specs=P(None, "slab", None, None),
        check_vma=False,
    )
```

```python
import math

import jax
import jax.numpy as jnp
import ml_dtypes
import numpy as np
from jax import lax
from jax.experimental import pallas as pl
from jax.experimental.pallas import tpu as pltpu
from jax.sharding import PartitionSpec as P

MIX = 0.5
NX = 2048
PW = 128
LANES = 128
TILES = NX // LANES
NZC = 8
NXL = 2
NXH = 2
NY = 4
ANGLES = NXH * NY
BLOCK = 16
HALF = NX // 2
CHUNK = NX // NY
FAR_FIRST = (4, 3, 5, 2, 6, 1, 7, 0)
VMEM = 16 * 1024 * 1024


def dft_tables():
    indices = np.arange(PW, dtype=np.int64)
    phases = (indices[:, None] * indices[None, :] % PW).astype(np.float64) * (2.0 * math.pi / PW)
    factor = 1.0 / math.sqrt(PW)
    re = (np.cos(phases) * factor).astype(ml_dtypes.bfloat16)
    im = (-np.sin(phases) * factor).astype(ml_dtypes.bfloat16)
    forward = np.block([[re, im], [-im, re]])
    inverse = np.block([[re, -im], [im, re]])
    return forward.astype(ml_dtypes.bfloat16), inverse.astype(ml_dtypes.bfloat16)


class Here:
    def __init__(self):
        s = lax.axis_index("slab")
        a = lax.axis_index("angle")
        self.a = a
        self.c = lax.rem(s, 2)
        self.xl = lax.rem(lax.div(s, 2), 2)
        self.zc = lax.div(s, 4)
        self.y = lax.rem(a, NY)
        self.xh = lax.div(a, NY)
        self.m = self.xl * NZC + self.zc

    def z_of(self, rel):
        return lax.rem(self.zc + rel, NZC)

    def y_of(self, rel):
        return lax.rem(self.y + rel, NY)

    def x_of(self, flip):
        return 1 - self.xl if flip else self.xl

    def chip(self, rel_z, flip_x):
        return self.device(zc=self.z_of(rel_z), xl=self.x_of(flip_x))

    def angle_peer(self, flip_xh, rel_y):
        return self.device(xh=1 - self.xh if flip_xh else self.xh, y=self.y_of(rel_y))

    def device(self, zc=None, xl=None, c=None, xh=None, y=None):
        zc = self.zc if zc is None else zc
        xl = self.xl if xl is None else xl
        c = self.c if c is None else c
        xh = self.xh if xh is None else xh
        y = self.y if y is None else y
        return {"slab": zc * 4 + xl * 2 + c, "angle": xh * NY + y}

    @property
    def sibling(self):
        return self.device(c=1 - self.c)

    def greet(self):
        peers = [self.sibling]
        peers += [self.chip(r, f) for f in (0, 1) for r in range(NZC) if r or f]
        peers += [self.angle_peer(f, r) for f in (0, 1) for r in range(NY) if r or f]
        barrier = pltpu.get_barrier_semaphore()
        for peer in peers:
            pl.semaphore_signal(barrier, 1, device_id=peer, device_id_type=pl.DeviceIdType.MESH)
        pl.semaphore_wait(barrier, len(peers))


def rows16(block):
    return pl.ds(pl.multiple_of(block * BLOCK, BLOCK), BLOCK)


def half_cols(core):
    return pl.ds(pl.multiple_of(core * HALF, HALF), HALF)


def chunk_cols(y):
    return pl.ds(pl.multiple_of(y * CHUNK, CHUNK), CHUNK)


def remote(src, dst, send, recv, to):
    return pltpu.make_async_remote_copy(
        src_ref=src,
        dst_ref=dst,
        send_sem=send,
        recv_sem=recv,
        device_id=to,
        device_id_type=pl.DeviceIdType.MESH,
    )


def shifted_tiles(tiles, start, count):
    first = lax.div(start, LANES)
    inner = lax.rem(start, LANES)
    need = min(count + 1, TILES)
    for stride in (8, 4, 2, 1):
        keep = min(need + stride - 1, TILES)
        bit = lax.rem(lax.div(first, stride), 2) == 1
        size = len(tiles)
        tiles = [lax.select_n(bit, tiles[j], tiles[(j + stride) % size]) for j in range(keep)]
    back = lax.rem(LANES - inner, LANES)
    lane = lax.broadcasted_iota(jnp.int32, (BLOCK, LANES), 1)
    stay = lane < LANES - inner
    turned = [pltpu.roll(tile.astype(jnp.float32), back, 1) for tile in tiles]
    return [jnp.where(stay, turned[j], turned[(j + 1) % need]) for j in range(count)]


def tiles_of(row):
    return [row[:, j * LANES : (j + 1) * LANES] for j in range(TILES)]


class Copies:
    def __init__(self, here):
        self.here = here
        self.sent = []

    def start(self, src, dst, send, recv, to):
        copy = remote(src, dst, send, recv, to)
        copy.start()
        self.sent.append(copy)

    def arrived(self, ref, recv):
        remote(ref, ref, recv, recv, self.here.sibling).wait_recv()

    def drain(self):
        for copy in self.sent:
            copy.wait_send()


def to_y(here, copies, piece, k, sems):
    send, recv = sems
    mine = piece(here.y)
    for d in (1, 3, 2):
        copies.start(mine, mine, send.at[d, k], recv.at[NY - d, k], here.angle_peer(0, d))


def from_y(here, copies, piece, k, sems):
    send, recv = sems
    for d in (1, 3, 2):
        copies.arrived(piece(here.y_of(d)), recv.at[d, k])


def project_kernel(
    vol, off, proj, offs_out, gath, acc, sib, offt, offv, offs_s,
    s_off, r_off, s_t1, r_t1, s_y, r_y, s_sib, r_sib, s_z, r_z, s_x, r_x, s_c, r_c, s_oa, r_oa, l_sem,
):
    here = Here()
    offt[here.m] = jnp.full((8, LANES), off[0, 0], jnp.int32)
    here.greet()
    copies = Copies(here)
    order = (0, 1, 7, 2, 6, 3, 5, 4)
    cols = chunk_cols(here.y)
    for rel in order:
        r = (NZC - rel) % NZC
        for f in (0, 1):
            if rel or f:
                to = here.chip(r, f)
                block = here.x_of(f) * NZC + here.z_of(r)
                copies.start(offt.at[here.m], offt.at[here.m], s_off.at[f, rel], r_off.at[f, rel], to)
                copies.start(
                    vol.at[rows16(block), cols], gath.at[f, rel, :, cols], s_t1.at[f, rel], r_t1.at[f, rel], to
                )
    own = pltpu.make_async_copy(vol.at[rows16(here.m)], gath.at[0, 0], l_sem.at[0])
    own.start()

    def piece(rel):
        if rel == 0:
            return lambda y: gath.at[1, 0, :, chunk_cols(y)]
        return lambda y: gath.at[:, rel, :, chunk_cols(y)]

    for rel in order:
        for f in (0, 1):
            if rel or f:
                copies.arrived(gath.at[f, rel, :, cols], r_t1.at[f, rel])
        to_y(here, copies, piece(rel), rel, (s_y, r_y))

    for f in (0, 1):
        for r in range(NZC):
            if r or f:
                copies.arrived(offt.at[here.x_of(f) * NZC + here.z_of(r)], r_off.at[f, r])
    for g in range(NXL * NZC):
        offv[g : g + 1, :] = offt[g, 0:1, :]
    down = pltpu.make_async_copy(offv, offs_s, l_sem.at[1])
    down.start()
    for f in (0, 1):
        for r in range(NY):
            if r or f:
                back = (NY - r) % NY
                copies.start(offv, offs_out.at[here.a], s_oa.at[f, r], r_oa.at[f, back], here.angle_peer(f, r))
    offs_out[here.a] = offv[...]
    down.wait()
    own.wait()
    acc[...] = jnp.zeros_like(acc)
    for rel in order:
        from_y(here, copies, piece(rel), rel, (s_y, r_y))

        def add_slot(f, carry):
            g = lax.rem(here.xl + f, NXL) * NZC + here.z_of(rel)
            for j, tile in enumerate(shifted_tiles(tiles_of(gath[f, rel]), offs_s[g, 0], TILES)):
                acc[:, j * LANES : (j + 1) * LANES] += tile
            return carry

        lax.fori_loop(0, NXL, add_slot, 0)

    mine, other = half_cols(here.c), half_cols(1 - here.c)
    copies.start(acc.at[:, other], sib, s_sib, r_sib, here.sibling)
    copies.arrived(sib, r_sib)
    proj[rows16(here.m), mine] = (acc[:, mine] + sib[...]).astype(jnp.bfloat16)

    own = proj.at[rows16(here.m), mine]
    for r in (1, 7, 2, 6, 3, 5, 4):
        copies.start(own, own, s_z.at[r], r_z.at[(NZC - r) % NZC], here.chip(r, 0))
    copies.start(own, own, s_x.at[0], r_x.at[0], here.chip(0, 1))
    copies.start(own, own, s_c.at[0, 0], r_c.at[0, 0], here.sibling)
    for rel in (1, 7, 2, 6, 3, 5, 4):
        got = proj.at[rows16(here.xl * NZC + here.z_of(rel)), mine]
        copies.arrived(got, r_z.at[rel])
        copies.start(got, got, s_x.at[rel], r_x.at[rel], here.chip(0, 1))
        copies.start(got, got, s_c.at[0, rel], r_c.at[0, rel], here.sibling)
    for rel in order:
        got = proj.at[rows16(here.x_of(1) * NZC + here.z_of(rel)), mine]
        copies.arrived(got, r_x.at[rel])
        copies.start(got, got, s_c.at[1, rel], r_c.at[1, rel], here.sibling)
    for f in (0, 1):
        for rel in order:
            copies.arrived(proj.at[rows16(here.x_of(f) * NZC + here.z_of(rel)), other], r_c.at[f, rel])
    for f in (0, 1):
        for r in range(NY):
            if r or f:
                a_from = (1 - here.xh if f else here.xh) * NY + here.y_of(r)
                copies.arrived(offs_out.at[a_from], r_oa.at[f, r])
    copies.drain()


GROUP = 8


def wave_kernel(proj, probe, measured, pos, forward, inverse, out, total):
    total[...] = jnp.zeros_like(total)
    count = measured.shape[1] // PW

    def swap(x):
        n = x.shape[0] // PW
        parts = [[x[k * PW : (k + 1) * PW, h * PW : (h + 1) * PW] for k in range(n)] for h in range(2)]
        return jnp.concatenate([jnp.concatenate(p, axis=1) for p in parts], axis=0)

    def one_group(group, carry):
        p_re = probe[0].astype(jnp.float32)
        p_im = probe[1].astype(jnp.float32)
        fwd = forward[...]
        inv = inverse[...]
        starts = []
        exits = []
        for k in range(GROUP):
            at = pos[GROUP * group + k]
            first = jnp.minimum(lax.div(at, LANES), TILES - 2)
            inner = at - first * LANES
            where = pl.ds(pl.multiple_of(first * LANES, LANES), 2 * LANES)
            starts.append((where, inner))
            row = lax.broadcasted_iota(jnp.int32, (2 * LANES, PW), 0)
            col = lax.broadcasted_iota(jnp.int32, (2 * LANES, PW), 1)
            pick = jnp.where(row == col + inner, 1.0, 0.0).astype(jnp.bfloat16)
            patch = jnp.dot(proj[:, where], pick, preferred_element_type=jnp.float32)
            re, im = patch[:PW], patch[PW:]
            exits.append(
                jnp.concatenate([p_re * re - p_im * im, p_re * im + p_im * re], axis=1).astype(jnp.bfloat16)
            )
        half = jnp.dot(jnp.concatenate(exits, axis=0), fwd, preferred_element_type=jnp.float32).astype(jnp.bfloat16)
        far = jnp.dot(inv, swap(half), preferred_element_type=jnp.float32)
        waves = []
        for k in range(GROUP):
            f_re = far[:PW, k * PW : (k + 1) * PW]
            f_im = far[PW:, k * PW : (k + 1) * PW]
            at = pl.multiple_of((GROUP * group + k) * PW, PW)
            target = measured[:, pl.ds(at, PW)].astype(jnp.float32)
            misfit = f_re * f_re + f_im * f_im - target
            waves.append(jnp.concatenate([misfit * f_re, misfit * f_im], axis=1).astype(jnp.bfloat16))
        back = jnp.dot(jnp.concatenate(waves, axis=0), inv, preferred_element_type=jnp.float32).astype(jnp.bfloat16)
        grad = jnp.dot(fwd, swap(back), preferred_element_type=jnp.float32)
        placed = []
        for k, (where, inner) in enumerate(starts):
            g_re = grad[:PW, k * PW : (k + 1) * PW]
            g_im = grad[PW:, k * PW : (k + 1) * PW]
            patch_grad = jnp.concatenate(
                [p_re * g_re + p_im * g_im, p_re * g_im - p_im * g_re], axis=0
            ).astype(jnp.bfloat16)
            row = lax.broadcasted_iota(jnp.int32, (PW, 2 * LANES), 0)
            col = lax.broadcasted_iota(jnp.int32, (PW, 2 * LANES), 1)
            put = jnp.where(col == row + inner, 1.0, 0.0).astype(jnp.bfloat16)
            placed.append(jnp.dot(patch_grad, put, preferred_element_type=jnp.float32))
        for (where, inner), value in zip(starts, placed):
            total[:, where] += value
        return carry

    lax.fori_loop(0, count // GROUP, one_group, 0)
    out[...] = total[...].astype(jnp.bfloat16)


def volume_kernel(
    part, offs, out, cbuf, xsend, xbuf, zsend, zbuf, dgall, vsend,
    s_c, r_c, s_x, r_x, s_z, r_z, s_a, r_a, s_s, r_s, s_v, r_v, s_y, r_y,
):
    here = Here()
    here.greet()
    copies = Copies(here)
    mine, other = half_cols(here.c), half_cols(1 - here.c)
    for f in (1, 0):
        for r in FAR_FIRST:
            src = part.at[rows16(here.x_of(f) * NZC + here.z_of(r)), other]
            copies.start(src, cbuf.at[f, r], s_c.at[f, r], r_c.at[f, r], here.sibling)
    for r in FAR_FIRST:
        copies.arrived(cbuf.at[1, r], r_c.at[1, r])
        own = part[rows16(here.x_of(1) * NZC + here.z_of(r)), mine]
        xsend[r] = (own.astype(jnp.float32) + cbuf[1, r].astype(jnp.float32)).astype(jnp.bfloat16)
        copies.start(xsend.at[r], xbuf.at[r], s_x.at[r], r_x.at[r], here.chip(0, 1))
    total = None
    for r in FAR_FIRST:
        copies.arrived(cbuf.at[0, r], r_c.at[0, r])
        own = part[rows16(here.xl * NZC + here.z_of(r)), mine]
        value = own.astype(jnp.float32) + cbuf[0, r].astype(jnp.float32)
        copies.arrived(xbuf.at[r], r_x.at[r])
        value = value + xbuf[r].astype(jnp.float32)
        if r:
            zsend[r] = value.astype(jnp.bfloat16)
            slot = (NZC - r) % NZC
            copies.start(zsend.at[r], zbuf.at[slot], s_z.at[r], r_z.at[slot], here.chip(r, 0))
        else:
            total = value
    for r in (1, 7, 2, 6, 3, 5, 4):
        copies.arrived(zbuf.at[r], r_z.at[r])
        total = total + zbuf[r].astype(jnp.float32)
    dgall[here.a, :, mine] = total.astype(jnp.bfloat16)
    own = dgall.at[here.a, :, mine]
    peers = [(0, 1), (0, 3), (1, 0), (0, 2), (1, 1), (1, 3), (1, 2)]
    for f, r in peers:
        copies.start(own, own, s_a.at[f, r], r_a.at[f, (NY - r) % NY], here.angle_peer(f, r))
    copies.start(own, own, s_s.at[0, 0], r_s.at[0, 0], here.sibling)

    def angle_of(f, r):
        return (1 - here.xh if f else here.xh) * NY + here.y_of(r)

    for f, r in peers:
        got = dgall.at[angle_of(f, r), :, mine]
        copies.arrived(got, r_a.at[f, r])
        copies.start(got, got, s_s.at[f, r], r_s.at[f, r], here.sibling)
    for f, r in [(0, 0)] + peers:
        copies.arrived(dgall.at[angle_of(f, r), :, other], r_s.at[f, r])

    cols = chunk_cols(here.y)
    zrows = rows16(here.zc)

    def gradient(f, r):
        g = here.x_of(f) * NZC + here.z_of(r)

        def add_angle(b, sums):
            first = lax.rem(here.y * CHUNK + NX - offs[b * NXL * NZC + g, 0], NX)
            tiles = shifted_tiles(tiles_of(dgall[b]), first, CHUNK // LANES)
            return [x + t for x, t in zip(sums, tiles)]

        sums = [jnp.zeros((BLOCK, LANES), jnp.float32)] * (CHUNK // LANES)
        sums = lax.fori_loop(0, ANGLES, add_angle, sums, unroll=2)
        return jnp.concatenate(sums, axis=1).astype(jnp.bfloat16)

    for r in FAR_FIRST:
        for f in (1, 0):
            value = gradient(f, r)
            if r or f:
                slot = (NZC - r) % NZC
                vsend[f, r] = value
                copies.start(
                    vsend.at[f, r], out.at[here.xl, zrows, cols], s_v.at[f, r], r_v.at[f, slot], here.chip(r, f)
                )
            else:
                out[here.xl, zrows, cols] = value

    def piece(rel):
        return lambda y: out.at[:, rows16(here.z_of(rel)), chunk_cols(y)]

    order = (0, 1, 7, 2, 6, 3, 5, 4)
    for rel in order:
        for f in (0, 1):
            if rel or f:
                copies.arrived(out.at[here.x_of(f), rows16(here.z_of(rel)), cols], r_v.at[f, rel])
        to_y(here, copies, piece(rel), rel, (s_y, r_y))
    for rel in order:
        from_y(here, copies, piece(rel), rel, (s_y, r_y))
    copies.drain()


def dma(*shape):
    return pltpu.SemaphoreType.DMA(shape)


def vmem():
    return pl.BlockSpec(memory_space=pltpu.VMEM)


def smem():
    return pl.BlockSpec(memory_space=pltpu.SMEM)


def project(lines, off):
    return pl.pallas_call(
        project_kernel,
        out_shape=(
            jax.ShapeDtypeStruct((2 * PW, NX), jnp.bfloat16),
            jax.ShapeDtypeStruct((ANGLES, NXL * NZC, LANES), jnp.int32),
        ),
        in_specs=[vmem(), smem()],
        out_specs=(vmem(), vmem()),
        scratch_shapes=[
            pltpu.VMEM((NXL, NZC, BLOCK, NX), jnp.bfloat16),
            pltpu.VMEM((BLOCK, NX), jnp.float32),
            pltpu.VMEM((BLOCK, HALF), jnp.float32),
            pltpu.VMEM((NXL * NZC, 8, LANES), jnp.int32),
            pltpu.VMEM((NXL * NZC, LANES), jnp.int32),
            pltpu.SMEM((NXL * NZC, LANES), jnp.int32),
            dma(NXL, NZC), dma(NXL, NZC), dma(NXL, NZC), dma(NXL, NZC),
            dma(NY, NZC), dma(NY, NZC),
            pltpu.SemaphoreType.DMA, pltpu.SemaphoreType.DMA,
            dma(NZC), dma(NZC), dma(NZC), dma(NZC),
            dma(NXL, NZC), dma(NXL, NZC),
            dma(NXH, NY), dma(NXH, NY),
            dma(2),
        ],
        compiler_params=pltpu.CompilerParams(collective_id=0, has_side_effects=True, vmem_limit_bytes=VMEM),
        name="project",
    )(lines, off)


def waves(proj, probe, measured, pos, forward, inverse):
    return pl.pallas_call(
        wave_kernel,
        out_shape=jax.ShapeDtypeStruct((2 * PW, NX), jnp.bfloat16),
        in_specs=[vmem(), vmem(), vmem(), smem(), vmem(), vmem()],
        out_specs=vmem(),
        scratch_shapes=[pltpu.VMEM((2 * PW, NX), jnp.float32)],
        compiler_params=pltpu.CompilerParams(vmem_limit_bytes=2 * VMEM),
        name="waves",
    )(proj, probe, measured, pos, forward, inverse)


def volume_gradient(part, offs):
    bf16 = jnp.bfloat16
    return pl.pallas_call(
        volume_kernel,
        out_shape=jax.ShapeDtypeStruct((2, PW, NX), bf16),
        in_specs=[vmem(), smem()],
        out_specs=vmem(),
        scratch_shapes=[
            pltpu.VMEM((NXL, NZC, BLOCK, HALF), bf16),
            pltpu.VMEM((NZC, BLOCK, HALF), bf16),
            pltpu.VMEM((NZC, BLOCK, HALF), bf16),
            pltpu.VMEM((NZC, BLOCK, HALF), bf16),
            pltpu.VMEM((NZC, BLOCK, HALF), bf16),
            pltpu.VMEM((ANGLES, BLOCK, NX), bf16),
            pltpu.VMEM((NXL, NZC, BLOCK, CHUNK), bf16),
            dma(NXL, NZC), dma(NXL, NZC),
            dma(NZC), dma(NZC), dma(NZC), dma(NZC),
            dma(NXH, NY), dma(NXH, NY), dma(NXH, NY), dma(NXH, NY),
            dma(NXL, NZC), dma(NXL, NZC),
            dma(NY, NZC), dma(NY, NZC),
        ],
        compiler_params=pltpu.CompilerParams(collective_id=1, has_side_effects=True, vmem_limit_bytes=VMEM),
        name="volume_gradient",
    )(part, offs)


def per_device(volume, consensus, probe, intensities, positions, offsets):
    pos_count = positions.shape[1]
    forward, inverse = dft_tables()
    lines = volume.reshape(2 * PW, NX)
    measured = intensities.reshape(PW, pos_count * PW)
    proj, offs = project(lines, offsets)
    part = waves(proj, probe, measured, positions.reshape(-1), jnp.asarray(forward), jnp.asarray(inverse))
    grad = volume_gradient(part, offs.reshape(ANGLES * NXL * NZC, LANES))
    rate = math.sqrt(NX / (pos_count * lax.axis_size("slab") * ANGLES * PW))
    current = volume.astype(jnp.float32)
    step = grad[:, None].astype(jnp.float32)
    return current - rate * step - MIX * (current - consensus.astype(jnp.float32))


def solution(mesh):
    return jax.shard_map(
        per_device,
        mesh=mesh,
        in_specs=(
            P(None, "slab", None, None),
            P(None, "slab", None, None),
            P(),
            P("angle", None, "slab", None),
            P("angle", "slab"),
            P("angle", "slab"),
        ),
        out_specs=P(None, "slab", None, None),
        check_vma=False,
    )
```

```python
import math

import jax
import jax.numpy as jnp
import ml_dtypes
import numpy as np
from jax import lax
from jax.experimental import pallas as pl
from jax.experimental.pallas import tpu as pltpu
from jax.sharding import PartitionSpec as P

MIX = 0.5
NX = 2048
PW = 128
LANES = 128
TILES = NX // LANES
NZC = 8
NXL = 2
NXH = 2
NY = 4
ANGLES = NXH * NY
BLOCK = 16
HALF = NX // 2
CHUNK = NX // NY
FAR_FIRST = (4, 3, 5, 2, 6, 1, 7, 0)
VMEM = 16 * 1024 * 1024


def dft_tables():
    indices = np.arange(PW, dtype=np.int64)
    phases = (indices[:, None] * indices[None, :] % PW).astype(np.float64) * (2.0 * math.pi / PW)
    factor = 1.0 / math.sqrt(PW)
    re = (np.cos(phases) * factor).astype(ml_dtypes.bfloat16)
    im = (-np.sin(phases) * factor).astype(ml_dtypes.bfloat16)
    forward = np.block([[re, im], [-im, re]])
    inverse = np.block([[re, -im], [im, re]])
    return forward.astype(ml_dtypes.bfloat16), inverse.astype(ml_dtypes.bfloat16)


class Here:
    def __init__(self):
        s = lax.axis_index("slab")
        a = lax.axis_index("angle")
        self.a = a
        self.c = lax.rem(s, 2)
        self.xl = lax.rem(lax.div(s, 2), 2)
        self.zc = lax.div(s, 4)
        self.y = lax.rem(a, NY)
        self.xh = lax.div(a, NY)
        self.m = self.xl * NZC + self.zc

    def z_of(self, rel):
        return lax.rem(self.zc + rel, NZC)

    def y_of(self, rel):
        return lax.rem(self.y + rel, NY)

    def x_of(self, flip):
        return 1 - self.xl if flip else self.xl

    def chip(self, rel_z, flip_x):
        return self.device(zc=self.z_of(rel_z), xl=self.x_of(flip_x))

    def angle_peer(self, flip_xh, rel_y):
        return self.device(xh=1 - self.xh if flip_xh else self.xh, y=self.y_of(rel_y))

    def device(self, zc=None, xl=None, c=None, xh=None, y=None):
        zc = self.zc if zc is None else zc
        xl = self.xl if xl is None else xl
        c = self.c if c is None else c
        xh = self.xh if xh is None else xh
        y = self.y if y is None else y
        return {"slab": zc * 4 + xl * 2 + c, "angle": xh * NY + y}

    @property
    def sibling(self):
        return self.device(c=1 - self.c)

    def greet(self):
        peers = [self.sibling]
        peers += [self.chip(r, f) for f in (0, 1) for r in range(NZC) if r or f]
        peers += [self.angle_peer(f, r) for f in (0, 1) for r in range(NY) if r or f]
        barrier = pltpu.get_barrier_semaphore()
        for peer in peers:
            pl.semaphore_signal(barrier, 1, device_id=peer, device_id_type=pl.DeviceIdType.MESH)
        pl.semaphore_wait(barrier, len(peers))


def rows16(block):
    return pl.ds(pl.multiple_of(block * BLOCK, BLOCK), BLOCK)


def half_cols(core):
    return pl.ds(pl.multiple_of(core * HALF, HALF), HALF)


def chunk_cols(y):
    return pl.ds(pl.multiple_of(y * CHUNK, CHUNK), CHUNK)


def remote(src, dst, send, recv, to):
    return pltpu.make_async_remote_copy(
        src_ref=src,
        dst_ref=dst,
        send_sem=send,
        recv_sem=recv,
        device_id=to,
        device_id_type=pl.DeviceIdType.MESH,
    )


def shifted_tiles(tiles, start, count):
    first = start >> 7
    inner = start & (LANES - 1)
    need = min(count + 1, TILES)
    for level in (3, 2, 1, 0):
        stride = 1 << level
        keep = min(need + stride - 1, TILES)
        bit = (first >> level) & 1 == 1
        size = len(tiles)
        tiles = [lax.select_n(bit, tiles[j], tiles[(j + stride) % size]) for j in range(keep)]
    back = (LANES - inner) & (LANES - 1)
    lane = lax.broadcasted_iota(jnp.int32, (BLOCK, LANES), 1)
    stay = lane < LANES - inner
    turned = [pltpu.roll(tile.astype(jnp.float32), back, 1) for tile in tiles]
    return [jnp.where(stay, turned[j], turned[(j + 1) % need]) for j in range(count)]


def tiles_of(row):
    return [row[:, j * LANES : (j + 1) * LANES] for j in range(TILES)]


class Copies:
    def __init__(self, here):
        self.here = here
        self.sent = []

    def start(self, src, dst, send, recv, to):
        copy = remote(src, dst, send, recv, to)
        copy.start()
        self.sent.append(copy)

    def arrived(self, ref, recv):
        remote(ref, ref, recv, recv, self.here.sibling).wait_recv()

    def drain(self):
        for copy in self.sent:
            copy.wait_send()


def to_y(here, copies, piece, k, sems):
    send, recv = sems
    mine = piece(here.y)
    for d in (1, 3, 2):
        copies.start(mine, mine, send.at[d, k], recv.at[NY - d, k], here.angle_peer(0, d))


def from_y(here, copies, piece, k, sems):
    send, recv = sems
    for d in (1, 3, 2):
        copies.arrived(piece(here.y_of(d)), recv.at[d, k])


def project_kernel(
    vol, off, proj, offs_out, gath, acc, sib, offt, offv, offs_s,
    s_off, r_off, s_t1, r_t1, s_y, r_y, s_sib, r_sib, s_z, r_z, s_x, r_x, s_c, r_c, s_oa, r_oa, l_sem,
):
    here = Here()
    offt[here.m] = jnp.full((8, LANES), off[0, 0], jnp.int32)
    here.greet()
    copies = Copies(here)
    order = (0, 1, 7, 2, 6, 3, 5, 4)
    cols = chunk_cols(here.y)
    for rel in order:
        r = (NZC - rel) % NZC
        for f in (0, 1):
            if rel or f:
                to = here.chip(r, f)
                block = here.x_of(f) * NZC + here.z_of(r)
                copies.start(offt.at[here.m], offt.at[here.m], s_off.at[f, rel], r_off.at[f, rel], to)
                copies.start(
                    vol.at[rows16(block), cols], gath.at[f, rel, :, cols], s_t1.at[f, rel], r_t1.at[f, rel], to
                )
    own = pltpu.make_async_copy(vol.at[rows16(here.m)], gath.at[0, 0], l_sem.at[0])
    own.start()

    def piece(rel):
        if rel == 0:
            return lambda y: gath.at[1, 0, :, chunk_cols(y)]
        return lambda y: gath.at[:, rel, :, chunk_cols(y)]

    for rel in order:
        for f in (0, 1):
            if rel or f:
                copies.arrived(gath.at[f, rel, :, cols], r_t1.at[f, rel])
        to_y(here, copies, piece(rel), rel, (s_y, r_y))

    for f in (0, 1):
        for r in range(NZC):
            if r or f:
                copies.arrived(offt.at[here.x_of(f) * NZC + here.z_of(r)], r_off.at[f, r])
    for g in range(NXL * NZC):
        offv[g : g + 1, :] = offt[g, 0:1, :]
    down = pltpu.make_async_copy(offv, offs_s, l_sem.at[1])
    down.start()
    for f in (0, 1):
        for r in range(NY):
            if r or f:
                back = (NY - r) % NY
                copies.start(offv, offs_out.at[here.a], s_oa.at[f, r], r_oa.at[f, back], here.angle_peer(f, r))
    offs_out[here.a] = offv[...]
    down.wait()
    own.wait()
    acc[...] = jnp.zeros_like(acc)
    for rel in order:
        from_y(here, copies, piece(rel), rel, (s_y, r_y))

        def add_slot(f, carry):
            g = lax.rem(here.xl + f, NXL) * NZC + here.z_of(rel)
            for j, tile in enumerate(shifted_tiles(tiles_of(gath[f, rel]), offs_s[g, 0], TILES)):
                acc[:, j * LANES : (j + 1) * LANES] += tile
            return carry

        lax.fori_loop(0, NXL, add_slot, 0)

    mine, other = half_cols(here.c), half_cols(1 - here.c)
    copies.start(acc.at[:, other], sib, s_sib, r_sib, here.sibling)
    copies.arrived(sib, r_sib)
    proj[rows16(here.m), mine] = (acc[:, mine] + sib[...]).astype(jnp.bfloat16)

    own = proj.at[rows16(here.m), mine]
    for r in (1, 7, 2, 6, 3, 5, 4):
        copies.start(own, own, s_z.at[r], r_z.at[(NZC - r) % NZC], here.chip(r, 0))
    copies.start(own, own, s_x.at[0], r_x.at[0], here.chip(0, 1))
    copies.start(own, own, s_c.at[0, 0], r_c.at[0, 0], here.sibling)
    for rel in (1, 7, 2, 6, 3, 5, 4):
        got = proj.at[rows16(here.xl * NZC + here.z_of(rel)), mine]
        copies.arrived(got, r_z.at[rel])
        copies.start(got, got, s_x.at[rel], r_x.at[rel], here.chip(0, 1))
        copies.start(got, got, s_c.at[0, rel], r_c.at[0, rel], here.sibling)
    for rel in order:
        got = proj.at[rows16(here.x_of(1) * NZC + here.z_of(rel)), mine]
        copies.arrived(got, r_x.at[rel])
        copies.start(got, got, s_c.at[1, rel], r_c.at[1, rel], here.sibling)
    for f in (0, 1):
        for rel in order:
            copies.arrived(proj.at[rows16(here.x_of(f) * NZC + here.z_of(rel)), other], r_c.at[f, rel])
    for f in (0, 1):
        for r in range(NY):
            if r or f:
                a_from = (1 - here.xh if f else here.xh) * NY + here.y_of(r)
                copies.arrived(offs_out.at[a_from], r_oa.at[f, r])
    copies.drain()


GROUP = 8


def wave_kernel(proj, probe, measured, pos, forward, inverse, out, total):
    total[...] = jnp.zeros_like(total)
    count = measured.shape[1] // PW

    def swap(x):
        n = x.shape[0] // PW
        parts = [[x[k * PW : (k + 1) * PW, h * PW : (h + 1) * PW] for k in range(n)] for h in range(2)]
        return jnp.concatenate([jnp.concatenate(p, axis=1) for p in parts], axis=0)

    def one_group(group, carry):
        p_re = probe[0].astype(jnp.float32)
        p_im = probe[1].astype(jnp.float32)
        fwd = forward[...]
        inv = inverse[...]
        starts = []
        exits = []
        for k in range(GROUP):
            at = pos[GROUP * group + k]
            first = jnp.minimum(lax.div(at, LANES), TILES - 2)
            inner = at - first * LANES
            where = pl.ds(pl.multiple_of(first * LANES, LANES), 2 * LANES)
            starts.append((where, inner))
            row = lax.broadcasted_iota(jnp.int32, (2 * LANES, PW), 0)
            col = lax.broadcasted_iota(jnp.int32, (2 * LANES, PW), 1)
            pick = jnp.where(row == col + inner, 1.0, 0.0).astype(jnp.bfloat16)
            patch = jnp.dot(proj[:, where], pick, preferred_element_type=jnp.float32)
            re, im = patch[:PW], patch[PW:]
            exits.append(
                jnp.concatenate([p_re * re - p_im * im, p_re * im + p_im * re], axis=1).astype(jnp.bfloat16)
            )
        half = jnp.dot(jnp.concatenate(exits, axis=0), fwd, preferred_element_type=jnp.float32).astype(jnp.bfloat16)
        far = jnp.dot(inv, swap(half), preferred_element_type=jnp.float32)
        waves = []
        for k in range(GROUP):
            f_re = far[:PW, k * PW : (k + 1) * PW]
            f_im = far[PW:, k * PW : (k + 1) * PW]
            at = pl.multiple_of((GROUP * group + k) * PW, PW)
            target = measured[:, pl.ds(at, PW)].astype(jnp.float32)
            misfit = f_re * f_re + f_im * f_im - target
            waves.append(jnp.concatenate([misfit * f_re, misfit * f_im], axis=1).astype(jnp.bfloat16))
        back = jnp.dot(jnp.concatenate(waves, axis=0), inv, preferred_element_type=jnp.float32).astype(jnp.bfloat16)
        grad = jnp.dot(fwd, swap(back), preferred_element_type=jnp.float32)
        placed = []
        for k, (where, inner) in enumerate(starts):
            g_re = grad[:PW, k * PW : (k + 1) * PW]
            g_im = grad[PW:, k * PW : (k + 1) * PW]
            patch_grad = jnp.concatenate(
                [p_re * g_re + p_im * g_im, p_re * g_im - p_im * g_re], axis=0
            ).astype(jnp.bfloat16)
            row = lax.broadcasted_iota(jnp.int32, (PW, 2 * LANES), 0)
            col = lax.broadcasted_iota(jnp.int32, (PW, 2 * LANES), 1)
            put = jnp.where(col == row + inner, 1.0, 0.0).astype(jnp.bfloat16)
            placed.append(jnp.dot(patch_grad, put, preferred_element_type=jnp.float32))
        for (where, inner), value in zip(starts, placed):
            total[:, where] += value
        return carry

    lax.fori_loop(0, count // GROUP, one_group, 0)
    out[...] = total[...].astype(jnp.bfloat16)


def volume_kernel(
    part, offs, out, cbuf, xsend, xbuf, zsend, zbuf, dgall, vsend,
    s_c, r_c, s_x, r_x, s_z, r_z, s_a, r_a, s_s, r_s, s_v, r_v, s_y, r_y,
):
    here = Here()
    here.greet()
    copies = Copies(here)
    mine, other = half_cols(here.c), half_cols(1 - here.c)
    for f in (1, 0):
        for r in FAR_FIRST:
            src = part.at[rows16(here.x_of(f) * NZC + here.z_of(r)), other]
            copies.start(src, cbuf.at[f, r], s_c.at[f, r], r_c.at[f, r], here.sibling)
    for r in FAR_FIRST:
        copies.arrived(cbuf.at[1, r], r_c.at[1, r])
        own = part[rows16(here.x_of(1) * NZC + here.z_of(r)), mine]
        xsend[r] = (own.astype(jnp.float32) + cbuf[1, r].astype(jnp.float32)).astype(jnp.bfloat16)
        copies.start(xsend.at[r], xbuf.at[r], s_x.at[r], r_x.at[r], here.chip(0, 1))
    total = None
    for r in FAR_FIRST:
        copies.arrived(cbuf.at[0, r], r_c.at[0, r])
        own = part[rows16(here.xl * NZC + here.z_of(r)), mine]
        value = own.astype(jnp.float32) + cbuf[0, r].astype(jnp.float32)
        copies.arrived(xbuf.at[r], r_x.at[r])
        value = value + xbuf[r].astype(jnp.float32)
        if r:
            zsend[r] = value.astype(jnp.bfloat16)
            slot = (NZC - r) % NZC
            copies.start(zsend.at[r], zbuf.at[slot], s_z.at[r], r_z.at[slot], here.chip(r, 0))
        else:
            total = value
    for r in (1, 7, 2, 6, 3, 5, 4):
        copies.arrived(zbuf.at[r], r_z.at[r])
        total = total + zbuf[r].astype(jnp.float32)
    dgall[here.a, :, mine] = total.astype(jnp.bfloat16)
    own = dgall.at[here.a, :, mine]
    peers = [(0, 1), (0, 3), (1, 0), (0, 2), (1, 1), (1, 3), (1, 2)]
    for f, r in peers:
        copies.start(own, own, s_a.at[f, r], r_a.at[f, (NY - r) % NY], here.angle_peer(f, r))
    copies.start(own, own, s_s.at[0, 0], r_s.at[0, 0], here.sibling)

    def angle_of(f, r):
        return (1 - here.xh if f else here.xh) * NY + here.y_of(r)

    for f, r in peers:
        got = dgall.at[angle_of(f, r), :, mine]
        copies.arrived(got, r_a.at[f, r])
        copies.start(got, got, s_s.at[f, r], r_s.at[f, r], here.sibling)
    for f, r in [(0, 0)] + peers:
        copies.arrived(dgall.at[angle_of(f, r), :, other], r_s.at[f, r])

    cols = chunk_cols(here.y)
    zrows = rows16(here.zc)

    def gradient(f, r):
        g = here.x_of(f) * NZC + here.z_of(r)
        sums = None
        for b in range(ANGLES):
            first = (here.y * CHUNK + NX - offs[b * NXL * NZC + g, 0]) & (NX - 1)
            tiles = shifted_tiles(tiles_of(dgall[b]), first, CHUNK // LANES)
            sums = tiles if sums is None else [x + t for x, t in zip(sums, tiles)]
        return jnp.concatenate(sums, axis=1).astype(jnp.bfloat16)

    order = (0, 1, 7, 2, 6, 3, 5, 4)
    for rel in order:
        r = (NZC - rel) % NZC
        for f in (0, 1):
            if r or f:
                vsend[f, r] = gradient(f, r)
                copies.start(
                    vsend.at[f, r], out.at[here.xl, zrows, cols], s_v.at[f, r], r_v.at[f, rel], here.chip(r, f)
                )
            else:
                out[here.xl, zrows, cols] = gradient(f, r)

    def piece(rel):
        return lambda y: out.at[:, rows16(here.z_of(rel)), chunk_cols(y)]

    for rel in order:
        for f in (0, 1):
            if rel or f:
                copies.arrived(out.at[here.x_of(f), rows16(here.z_of(rel)), cols], r_v.at[f, rel])
        to_y(here, copies, piece(rel), rel, (s_y, r_y))
    for rel in order:
        from_y(here, copies, piece(rel), rel, (s_y, r_y))
    copies.drain()


def dma(*shape):
    return pltpu.SemaphoreType.DMA(shape)


def vmem():
    return pl.BlockSpec(memory_space=pltpu.VMEM)


def smem():
    return pl.BlockSpec(memory_space=pltpu.SMEM)


def project(lines, off):
    return pl.pallas_call(
        project_kernel,
        out_shape=(
            jax.ShapeDtypeStruct((2 * PW, NX), jnp.bfloat16),
            jax.ShapeDtypeStruct((ANGLES, NXL * NZC, LANES), jnp.int32),
        ),
        in_specs=[vmem(), smem()],
        out_specs=(vmem(), vmem()),
        scratch_shapes=[
            pltpu.VMEM((NXL, NZC, BLOCK, NX), jnp.bfloat16),
            pltpu.VMEM((BLOCK, NX), jnp.float32),
            pltpu.VMEM((BLOCK, HALF), jnp.float32),
            pltpu.VMEM((NXL * NZC, 8, LANES), jnp.int32),
            pltpu.VMEM((NXL * NZC, LANES), jnp.int32),
            pltpu.SMEM((NXL * NZC, LANES), jnp.int32),
            dma(NXL, NZC), dma(NXL, NZC), dma(NXL, NZC), dma(NXL, NZC),
            dma(NY, NZC), dma(NY, NZC),
            pltpu.SemaphoreType.DMA, pltpu.SemaphoreType.DMA,
            dma(NZC), dma(NZC), dma(NZC), dma(NZC),
            dma(NXL, NZC), dma(NXL, NZC),
            dma(NXH, NY), dma(NXH, NY),
            dma(2),
        ],
        compiler_params=pltpu.CompilerParams(collective_id=0, has_side_effects=True, vmem_limit_bytes=VMEM),
        name="project",
    )(lines, off)


def waves(proj, probe, measured, pos, forward, inverse):
    return pl.pallas_call(
        wave_kernel,
        out_shape=jax.ShapeDtypeStruct((2 * PW, NX), jnp.bfloat16),
        in_specs=[vmem(), vmem(), vmem(), smem(), vmem(), vmem()],
        out_specs=vmem(),
        scratch_shapes=[pltpu.VMEM((2 * PW, NX), jnp.float32)],
        compiler_params=pltpu.CompilerParams(vmem_limit_bytes=2 * VMEM),
        name="waves",
    )(proj, probe, measured, pos, forward, inverse)


def volume_gradient(part, offs):
    bf16 = jnp.bfloat16
    return pl.pallas_call(
        volume_kernel,
        out_shape=jax.ShapeDtypeStruct((2, PW, NX), bf16),
        in_specs=[vmem(), smem()],
        out_specs=vmem(),
        scratch_shapes=[
            pltpu.VMEM((NXL, NZC, BLOCK, HALF), bf16),
            pltpu.VMEM((NZC, BLOCK, HALF), bf16),
            pltpu.VMEM((NZC, BLOCK, HALF), bf16),
            pltpu.VMEM((NZC, BLOCK, HALF), bf16),
            pltpu.VMEM((NZC, BLOCK, HALF), bf16),
            pltpu.VMEM((ANGLES, BLOCK, NX), bf16),
            pltpu.VMEM((NXL, NZC, BLOCK, CHUNK), bf16),
            dma(NXL, NZC), dma(NXL, NZC),
            dma(NZC), dma(NZC), dma(NZC), dma(NZC),
            dma(NXH, NY), dma(NXH, NY), dma(NXH, NY), dma(NXH, NY),
            dma(NXL, NZC), dma(NXL, NZC),
            dma(NY, NZC), dma(NY, NZC),
        ],
        compiler_params=pltpu.CompilerParams(collective_id=1, has_side_effects=True, vmem_limit_bytes=VMEM),
        name="volume_gradient",
    )(part, offs)


def per_device(volume, consensus, probe, intensities, positions, offsets):
    pos_count = positions.shape[1]
    forward, inverse = dft_tables()
    lines = volume.reshape(2 * PW, NX)
    measured = intensities.reshape(PW, pos_count * PW)
    proj, offs = project(lines, offsets)
    part = waves(proj, probe, measured, positions.reshape(-1), jnp.asarray(forward), jnp.asarray(inverse))
    grad = volume_gradient(part, offs.reshape(ANGLES * NXL * NZC, LANES))
    rate = math.sqrt(NX / (pos_count * lax.axis_size("slab") * ANGLES * PW))
    current = volume.astype(jnp.float32)
    step = grad[:, None].astype(jnp.float32)
    return current - rate * step - MIX * (current - consensus.astype(jnp.float32))


def solution(mesh):
    return jax.shard_map(
        per_device,
        mesh=mesh,
        in_specs=(
            P(None, "slab", None, None),
            P(None, "slab", None, None),
            P(),
            P("angle", None, "slab", None),
            P("angle", "slab"),
            P("angle", "slab"),
        ),
        out_specs=P(None, "slab", None, None),
        check_vma=False,
    )
```

```python
import math

import jax
import jax.numpy as jnp
import ml_dtypes
import numpy as np
from jax import lax
from jax.experimental import pallas as pl
from jax.experimental.pallas import tpu as pltpu
from jax.sharding import PartitionSpec as P

MIX = 0.5
NX = 2048
PW = 128
LANES = 128
TILES = NX // LANES
NZC = 8
NXL = 2
NXH = 2
NY = 4
ANGLES = NXH * NY
BLOCK = 16
HALF = NX // 2
CHUNK = NX // NY
FAR_FIRST = (4, 3, 5, 2, 6, 1, 7, 0)
VMEM = 16 * 1024 * 1024


def dft_tables():
    indices = np.arange(PW, dtype=np.int64)
    phases = (indices[:, None] * indices[None, :] % PW).astype(np.float64) * (2.0 * math.pi / PW)
    factor = 1.0 / math.sqrt(PW)
    re = (np.cos(phases) * factor).astype(ml_dtypes.bfloat16)
    im = (-np.sin(phases) * factor).astype(ml_dtypes.bfloat16)
    forward = np.block([[re, im], [-im, re]])
    inverse = np.block([[re, -im], [im, re]])
    return forward.astype(ml_dtypes.bfloat16), inverse.astype(ml_dtypes.bfloat16)


class Here:
    def __init__(self):
        s = lax.axis_index("slab")
        a = lax.axis_index("angle")
        self.a = a
        self.c = lax.rem(s, 2)
        self.xl = lax.rem(lax.div(s, 2), 2)
        self.zc = lax.div(s, 4)
        self.y = lax.rem(a, NY)
        self.xh = lax.div(a, NY)
        self.m = self.xl * NZC + self.zc

    def z_of(self, rel):
        return lax.rem(self.zc + rel, NZC)

    def y_of(self, rel):
        return lax.rem(self.y + rel, NY)

    def x_of(self, flip):
        return 1 - self.xl if flip else self.xl

    def chip(self, rel_z, flip_x):
        return self.device(zc=self.z_of(rel_z), xl=self.x_of(flip_x))

    def angle_peer(self, flip_xh, rel_y):
        return self.device(xh=1 - self.xh if flip_xh else self.xh, y=self.y_of(rel_y))

    def device(self, zc=None, xl=None, c=None, xh=None, y=None):
        zc = self.zc if zc is None else zc
        xl = self.xl if xl is None else xl
        c = self.c if c is None else c
        xh = self.xh if xh is None else xh
        y = self.y if y is None else y
        return {"slab": zc * 4 + xl * 2 + c, "angle": xh * NY + y}

    @property
    def sibling(self):
        return self.device(c=1 - self.c)

    def greet(self):
        peers = [self.sibling]
        peers += [self.chip(r, f) for f in (0, 1) for r in range(NZC) if r or f]
        peers += [self.angle_peer(f, r) for f in (0, 1) for r in range(NY) if r or f]
        barrier = pltpu.get_barrier_semaphore()
        for peer in peers:
            pl.semaphore_signal(barrier, 1, device_id=peer, device_id_type=pl.DeviceIdType.MESH)
        pl.semaphore_wait(barrier, len(peers))


def rows16(block):
    return pl.ds(pl.multiple_of(block * BLOCK, BLOCK), BLOCK)


def half_cols(core):
    return pl.ds(pl.multiple_of(core * HALF, HALF), HALF)


def chunk_cols(y):
    return pl.ds(pl.multiple_of(y * CHUNK, CHUNK), CHUNK)


def remote(src, dst, send, recv, to):
    return pltpu.make_async_remote_copy(
        src_ref=src,
        dst_ref=dst,
        send_sem=send,
        recv_sem=recv,
        device_id=to,
        device_id_type=pl.DeviceIdType.MESH,
    )


def shifted_tiles(tiles, start, count):
    first = start >> 7
    inner = start & (LANES - 1)
    need = min(count + 1, TILES)
    for level in (3, 2, 1, 0):
        stride = 1 << level
        keep = min(need + stride - 1, TILES)
        bit = (first >> level) & 1 == 1
        size = len(tiles)
        tiles = [lax.select_n(bit, tiles[j], tiles[(j + stride) % size]) for j in range(keep)]
    back = (LANES - inner) & (LANES - 1)
    lane = lax.broadcasted_iota(jnp.int32, (BLOCK, LANES), 1)
    stay = lane < LANES - inner
    turned = [pltpu.roll(tile.astype(jnp.float32), back, 1) for tile in tiles]
    return [jnp.where(stay, turned[j], turned[(j + 1) % need]) for j in range(count)]


def tiles_of(row):
    return [row[:, j * LANES : (j + 1) * LANES] for j in range(TILES)]


class Copies:
    def __init__(self, here):
        self.here = here
        self.sent = []

    def start(self, src, dst, send, recv, to):
        copy = remote(src, dst, send, recv, to)
        copy.start()
        self.sent.append(copy)

    def arrived(self, ref, recv):
        remote(ref, ref, recv, recv, self.here.sibling).wait_recv()

    def drain(self):
        for copy in self.sent:
            copy.wait_send()


WHOLE = ((1, 0), (0, 7), (0, 1))
PIECES = ((7, (1,)), (1, (1,)), (2, (0, 1)), (6, (0, 1)), (3, (0, 1)), (5, (0, 1)), (4, (0, 1)))


def to_y(here, copies, piece, k, sems):
    send, recv = sems
    mine = piece(here.y)
    for d in (2, 1, 3):
        copies.start(mine, mine, send.at[d, k], recv.at[NY - d, k], here.angle_peer(0, d))


def from_y(here, copies, piece, k, sems):
    send, recv = sems
    for d in (1, 3, 2):
        copies.arrived(piece(here.y_of(d)), recv.at[d, k])


def project_kernel(
    vol, off, proj, offs_out, gath, acc, sib, offt, offv, off_s, offs_s,
    s_off, r_off, s_t1, r_t1, s_y, r_y, s_sib, r_sib, s_z, r_z, s_x, r_x, s_c, r_c, s_oa, r_oa, l_sem,
):
    here = Here()
    fetch = pltpu.make_async_copy(off, off_s, l_sem.at[2])
    fetch.start()
    here.greet()
    copies = Copies(here)
    order = (0, 1, 7, 2, 6, 3, 5, 4)
    cols = chunk_cols(here.y)

    def send_block(f, rel, where):
        r = (NZC - rel) % NZC
        to = here.chip(r, f)
        block = here.x_of(f) * NZC + here.z_of(r)
        copies.start(vol.at[rows16(block), where], gath.at[f, rel, :, where], s_t1.at[f, rel], r_t1.at[f, rel], to)

    for rel, flips in PIECES:
        for f in flips:
            send_block(f, rel, cols)
    for f, rel in WHOLE:
        send_block(f, rel, slice(None))
    own = pltpu.make_async_copy(vol.at[rows16(here.m)], gath.at[0, 0], l_sem.at[0])
    own.start()
    fetch.wait()
    offt[here.m] = jnp.full((1, LANES), off_s[0, 0], jnp.int32)
    for rel in order:
        for f in (0, 1):
            if rel or f:
                to = here.chip((NZC - rel) % NZC, f)
                copies.start(offt.at[here.m], offt.at[here.m], s_off.at[f, rel], r_off.at[f, rel], to)

    def piece(rel, flips):
        f = slice(None) if len(flips) == 2 else flips[0]
        return lambda y: gath.at[f, rel, :, chunk_cols(y)]

    for rel, flips in PIECES:
        for f in flips:
            copies.arrived(gath.at[f, rel, :, cols], r_t1.at[f, rel])
        to_y(here, copies, piece(rel, flips), rel, (s_y, r_y))

    for f in (0, 1):
        for r in range(NZC):
            if r or f:
                copies.arrived(offt.at[here.x_of(f) * NZC + here.z_of(r)], r_off.at[f, r])
    lane = lax.broadcasted_iota(jnp.int32, (1, LANES), 1)
    packed = jnp.zeros((1, LANES), jnp.int32)
    for g in range(NXL * NZC):
        packed = jnp.where(lane == g, offt[g], packed)
    offv[...] = packed
    down = pltpu.make_async_copy(offv, offs_s, l_sem.at[1])
    down.start()
    for f in (0, 1):
        for r in range(NY):
            if r or f:
                back = (NY - r) % NY
                copies.start(offv, offs_out.at[here.a], s_oa.at[f, r], r_oa.at[f, back], here.angle_peer(f, r))
    offs_out[here.a] = packed
    down.wait()
    own.wait()
    acc[...] = jnp.zeros_like(acc)

    def add_slot(f, rel):
        g = lax.rem(here.xl + f, NXL) * NZC + here.z_of(rel)
        for j, tile in enumerate(shifted_tiles(tiles_of(gath[f, rel]), offs_s[0, g], TILES)):
            acc[:, j * LANES : (j + 1) * LANES] += tile

    add_slot(0, 0)
    for f, rel in WHOLE:
        copies.arrived(gath.at[f, rel], r_t1.at[f, rel])
        add_slot(f, rel)
    for rel, flips in PIECES:
        from_y(here, copies, piece(rel, flips), rel, (s_y, r_y))
        for f in flips:
            add_slot(f, rel)

    mine, other = half_cols(here.c), half_cols(1 - here.c)
    copies.start(acc.at[:, other], sib, s_sib, r_sib, here.sibling)
    copies.arrived(sib, r_sib)
    proj[rows16(here.m), mine] = (acc[:, mine] + sib[...]).astype(jnp.bfloat16)

    own = proj.at[rows16(here.m), mine]
    for r in (1, 7, 2, 6, 3, 5, 4):
        copies.start(own, own, s_z.at[r], r_z.at[(NZC - r) % NZC], here.chip(r, 0))
    copies.start(own, own, s_x.at[0], r_x.at[0], here.chip(0, 1))
    copies.start(own, own, s_c.at[0, 0], r_c.at[0, 0], here.sibling)
    for rel in (1, 7, 2, 6, 3, 5, 4):
        got = proj.at[rows16(here.xl * NZC + here.z_of(rel)), mine]
        copies.arrived(got, r_z.at[rel])
        copies.start(got, got, s_x.at[rel], r_x.at[rel], here.chip(0, 1))
        copies.start(got, got, s_c.at[0, rel], r_c.at[0, rel], here.sibling)
    for rel in order:
        got = proj.at[rows16(here.x_of(1) * NZC + here.z_of(rel)), mine]
        copies.arrived(got, r_x.at[rel])
        copies.start(got, got, s_c.at[1, rel], r_c.at[1, rel], here.sibling)
    for f in (0, 1):
        for rel in order:
            copies.arrived(proj.at[rows16(here.x_of(f) * NZC + here.z_of(rel)), other], r_c.at[f, rel])
    for f in (0, 1):
        for r in range(NY):
            if r or f:
                a_from = (1 - here.xh if f else here.xh) * NY + here.y_of(r)
                copies.arrived(offs_out.at[a_from], r_oa.at[f, r])
    copies.drain()


GROUP = 8


def wave_kernel(proj, probe, measured, pos, forward, inverse, out, total):
    total[...] = jnp.zeros_like(total)
    count = measured.shape[1] // PW

    def swap(x):
        n = x.shape[0] // PW
        parts = [[x[k * PW : (k + 1) * PW, h * PW : (h + 1) * PW] for k in range(n)] for h in range(2)]
        return jnp.concatenate([jnp.concatenate(p, axis=1) for p in parts], axis=0)

    def one_group(group, carry):
        p_re = probe[0].astype(jnp.float32)
        p_im = probe[1].astype(jnp.float32)
        fwd = forward[...]
        inv = inverse[...]
        starts = []
        exits = []
        for k in range(GROUP):
            at = pos[GROUP * group + k]
            first = jnp.minimum(lax.div(at, LANES), TILES - 2)
            inner = at - first * LANES
            where = pl.ds(pl.multiple_of(first * LANES, LANES), 2 * LANES)
            starts.append((where, inner))
            row = lax.broadcasted_iota(jnp.int32, (2 * LANES, PW), 0)
            col = lax.broadcasted_iota(jnp.int32, (2 * LANES, PW), 1)
            pick = jnp.where(row == col + inner, 1.0, 0.0).astype(jnp.bfloat16)
            patch = jnp.dot(proj[:, where], pick, preferred_element_type=jnp.float32)
            re, im = patch[:PW], patch[PW:]
            exits.append(
                jnp.concatenate([p_re * re - p_im * im, p_re * im + p_im * re], axis=1).astype(jnp.bfloat16)
            )
        half = jnp.dot(jnp.concatenate(exits, axis=0), fwd, preferred_element_type=jnp.float32).astype(jnp.bfloat16)
        far = jnp.dot(inv, swap(half), preferred_element_type=jnp.float32)
        waves = []
        for k in range(GROUP):
            f_re = far[:PW, k * PW : (k + 1) * PW]
            f_im = far[PW:, k * PW : (k + 1) * PW]
            at = pl.multiple_of((GROUP * group + k) * PW, PW)
            target = measured[:, pl.ds(at, PW)].astype(jnp.float32)
            misfit = f_re * f_re + f_im * f_im - target
            waves.append(jnp.concatenate([misfit * f_re, misfit * f_im], axis=1).astype(jnp.bfloat16))
        back = jnp.dot(jnp.concatenate(waves, axis=0), inv, preferred_element_type=jnp.float32).astype(jnp.bfloat16)
        grad = jnp.dot(fwd, swap(back), preferred_element_type=jnp.float32)
        placed = []
        for k, (where, inner) in enumerate(starts):
            g_re = grad[:PW, k * PW : (k + 1) * PW]
            g_im = grad[PW:, k * PW : (k + 1) * PW]
            patch_grad = jnp.concatenate(
                [p_re * g_re + p_im * g_im, p_re * g_im - p_im * g_re], axis=0
            ).astype(jnp.bfloat16)
            row = lax.broadcasted_iota(jnp.int32, (PW, 2 * LANES), 0)
            col = lax.broadcasted_iota(jnp.int32, (PW, 2 * LANES), 1)
            put = jnp.where(col == row + inner, 1.0, 0.0).astype(jnp.bfloat16)
            placed.append(jnp.dot(patch_grad, put, preferred_element_type=jnp.float32))
        for (where, inner), value in zip(starts, placed):
            total[:, where] += value
        return carry

    lax.fori_loop(0, count // GROUP, one_group, 0)
    out[...] = total[...].astype(jnp.bfloat16)


def volume_kernel(
    part, offs, out, cbuf, xsend, xbuf, zsend, zbuf, dgall, vsend,
    s_c, r_c, s_x, r_x, s_z, r_z, s_a, r_a, s_s, r_s, s_v, r_v, s_y, r_y,
):
    here = Here()
    here.greet()
    copies = Copies(here)
    mine, other = half_cols(here.c), half_cols(1 - here.c)
    for f in (1, 0):
        for r in FAR_FIRST:
            src = part.at[rows16(here.x_of(f) * NZC + here.z_of(r)), other]
            copies.start(src, cbuf.at[f, r], s_c.at[f, r], r_c.at[f, r], here.sibling)
    for r in FAR_FIRST:
        copies.arrived(cbuf.at[1, r], r_c.at[1, r])
        own = part[rows16(here.x_of(1) * NZC + here.z_of(r)), mine]
        xsend[r] = (own.astype(jnp.float32) + cbuf[1, r].astype(jnp.float32)).astype(jnp.bfloat16)
        copies.start(xsend.at[r], xbuf.at[r], s_x.at[r], r_x.at[r], here.chip(0, 1))
    total = None
    for r in FAR_FIRST:
        copies.arrived(cbuf.at[0, r], r_c.at[0, r])
        own = part[rows16(here.xl * NZC + here.z_of(r)), mine]
        value = own.astype(jnp.float32) + cbuf[0, r].astype(jnp.float32)
        copies.arrived(xbuf.at[r], r_x.at[r])
        value = value + xbuf[r].astype(jnp.float32)
        if r:
            zsend[r] = value.astype(jnp.bfloat16)
            slot = (NZC - r) % NZC
            copies.start(zsend.at[r], zbuf.at[slot], s_z.at[r], r_z.at[slot], here.chip(r, 0))
        else:
            total = value
    for r in (1, 7, 2, 6, 3, 5, 4):
        copies.arrived(zbuf.at[r], r_z.at[r])
        total = total + zbuf[r].astype(jnp.float32)
    dgall[here.a, :, mine] = total.astype(jnp.bfloat16)
    own = dgall.at[here.a, :, mine]
    peers = [(0, 1), (0, 3), (1, 0), (0, 2), (1, 1), (1, 3), (1, 2)]
    for f, r in peers:
        copies.start(own, own, s_a.at[f, r], r_a.at[f, (NY - r) % NY], here.angle_peer(f, r))
    copies.start(own, own, s_s.at[0, 0], r_s.at[0, 0], here.sibling)

    def angle_of(f, r):
        return (1 - here.xh if f else here.xh) * NY + here.y_of(r)

    for f, r in peers:
        got = dgall.at[angle_of(f, r), :, mine]
        copies.arrived(got, r_a.at[f, r])
        copies.start(got, got, s_s.at[f, r], r_s.at[f, r], here.sibling)
    for f, r in [(0, 0)] + peers:
        copies.arrived(dgall.at[angle_of(f, r), :, other], r_s.at[f, r])

    cols = chunk_cols(here.y)
    zrows = rows16(here.zc)

    def gradient(f, rel, start, count):
        g = here.x_of(f) * NZC + here.z_of((NZC - rel) % NZC)
        sums = None
        for b in range(ANGLES):
            first = (start + NX - offs[b, g]) & (NX - 1)
            tiles = shifted_tiles(tiles_of(dgall[b]), first, count)
            sums = tiles if sums is None else [x + t for x, t in zip(sums, tiles)]
        return jnp.concatenate(sums, axis=1).astype(jnp.bfloat16)

    def send_block(f, rel, where):
        copies.start(
            vsend.at[f, rel, :, where],
            out.at[here.xl, zrows, where],
            s_v.at[f, rel],
            r_v.at[f, rel],
            here.chip((NZC - rel) % NZC, f),
        )

    for rel, flips in PIECES:
        for f in flips:
            vsend[f, rel, :, cols] = gradient(f, rel, here.y * CHUNK, CHUNK // LANES)
            send_block(f, rel, cols)
    for f, rel in WHOLE:
        vsend[f, rel] = gradient(f, rel, 0, TILES)
        send_block(f, rel, slice(None))
    out[here.xl, zrows, :] = gradient(0, 0, 0, TILES)

    def piece(rel, flips):
        f = slice(None) if len(flips) == 2 else here.x_of(flips[0])
        return lambda y: out.at[f, rows16(here.z_of(rel)), chunk_cols(y)]

    for rel, flips in PIECES:
        for f in flips:
            copies.arrived(out.at[here.x_of(f), rows16(here.z_of(rel)), cols], r_v.at[f, rel])
        to_y(here, copies, piece(rel, flips), rel, (s_y, r_y))
    for f, rel in WHOLE:
        copies.arrived(out.at[here.x_of(f), rows16(here.z_of(rel))], r_v.at[f, rel])
    for rel, flips in PIECES:
        from_y(here, copies, piece(rel, flips), rel, (s_y, r_y))
    copies.drain()


def dma(*shape):
    return pltpu.SemaphoreType.DMA(shape)


def vmem():
    return pl.BlockSpec(memory_space=pltpu.VMEM)


def smem():
    return pl.BlockSpec(memory_space=pltpu.SMEM)


def project(lines, off):
    return pl.pallas_call(
        project_kernel,
        out_shape=(
            jax.ShapeDtypeStruct((2 * PW, NX), jnp.bfloat16),
            jax.ShapeDtypeStruct((ANGLES, 1, LANES), jnp.int32),
        ),
        in_specs=[pl.BlockSpec(memory_space=pl.ANY), pl.BlockSpec(memory_space=pl.ANY)],
        out_specs=(vmem(), vmem()),
        scratch_shapes=[
            pltpu.VMEM((NXL, NZC, BLOCK, NX), jnp.bfloat16),
            pltpu.VMEM((BLOCK, NX), jnp.float32),
            pltpu.VMEM((BLOCK, HALF), jnp.float32),
            pltpu.VMEM((NXL * NZC, 1, LANES), jnp.int32),
            pltpu.VMEM((1, LANES), jnp.int32),
            pltpu.SMEM((1, 1), jnp.int32),
            pltpu.SMEM((1, LANES), jnp.int32),
            dma(NXL, NZC), dma(NXL, NZC), dma(NXL, NZC), dma(NXL, NZC),
            dma(NY, NZC), dma(NY, NZC),
            pltpu.SemaphoreType.DMA, pltpu.SemaphoreType.DMA,
            dma(NZC), dma(NZC), dma(NZC), dma(NZC),
            dma(NXL, NZC), dma(NXL, NZC),
            dma(NXH, NY), dma(NXH, NY),
            dma(3),
        ],
        compiler_params=pltpu.CompilerParams(collective_id=0, has_side_effects=True, vmem_limit_bytes=52 * 1024 * 1024),
        name="project",
    )(lines, off)


def waves(proj, probe, measured, pos, forward, inverse):
    return pl.pallas_call(
        wave_kernel,
        out_shape=jax.ShapeDtypeStruct((2 * PW, NX), jnp.bfloat16),
        in_specs=[vmem(), vmem(), vmem(), smem(), vmem(), vmem()],
        out_specs=vmem(),
        scratch_shapes=[pltpu.VMEM((2 * PW, NX), jnp.float32)],
        compiler_params=pltpu.CompilerParams(vmem_limit_bytes=2 * VMEM),
        name="waves",
    )(proj, probe, measured, pos, forward, inverse)


def volume_gradient(part, offs):
    bf16 = jnp.bfloat16
    return pl.pallas_call(
        volume_kernel,
        out_shape=jax.ShapeDtypeStruct((2, PW, NX), bf16),
        in_specs=[vmem(), smem()],
        out_specs=vmem(),
        scratch_shapes=[
            pltpu.VMEM((NXL, NZC, BLOCK, HALF), bf16),
            pltpu.VMEM((NZC, BLOCK, HALF), bf16),
            pltpu.VMEM((NZC, BLOCK, HALF), bf16),
            pltpu.VMEM((NZC, BLOCK, HALF), bf16),
            pltpu.VMEM((NZC, BLOCK, HALF), bf16),
            pltpu.VMEM((ANGLES, BLOCK, NX), bf16),
            pltpu.VMEM((NXL, NZC, BLOCK, NX), bf16),
            dma(NXL, NZC), dma(NXL, NZC),
            dma(NZC), dma(NZC), dma(NZC), dma(NZC),
            dma(NXH, NY), dma(NXH, NY), dma(NXH, NY), dma(NXH, NY),
            dma(NXL, NZC), dma(NXL, NZC),
            dma(NY, NZC), dma(NY, NZC),
        ],
        compiler_params=pltpu.CompilerParams(collective_id=1, has_side_effects=True, vmem_limit_bytes=VMEM),
        name="volume_gradient",
    )(part, offs)


def per_device(volume, consensus, probe, intensities, positions, offsets):
    pos_count = positions.shape[1]
    forward, inverse = dft_tables()
    lines = volume.reshape(2 * PW, NX)
    measured = intensities.reshape(PW, pos_count * PW)
    proj, offs = project(lines, offsets)
    part = waves(proj, probe, measured, positions.reshape(-1), jnp.asarray(forward), jnp.asarray(inverse))
    grad = volume_gradient(part, offs.reshape(ANGLES, LANES))
    rate = math.sqrt(NX / (pos_count * lax.axis_size("slab") * ANGLES * PW))
    current = volume.astype(jnp.float32)
    step = grad[:, None].astype(jnp.float32)
    return current - rate * step - MIX * (current - consensus.astype(jnp.float32))


def solution(mesh):
    return jax.shard_map(
        per_device,
        mesh=mesh,
        in_specs=(
            P(None, "slab", None, None),
            P(None, "slab", None, None),
            P(),
            P("angle", None, "slab", None),
            P("angle", "slab"),
            P("angle", "slab"),
        ),
        out_specs=P(None, "slab", None, None),
        check_vma=False,
    )
```

```python
import functools
import math

import jax
import jax.numpy as jnp
import ml_dtypes
import numpy as np
from jax import lax
from jax.experimental import pallas as pl
from jax.experimental.pallas import tpu as pltpu
from jax.sharding import PartitionSpec as P

MIX = 0.5
NX = 2048
PW = 128
LANES = 128
TILES = NX // LANES
NZC = 8
NXL = 2
NXH = 2
NY = 4
ANGLES = NXH * NY
BLOCK = 16
HALF = NX // 2
CHUNK = NX // NY
FAR_FIRST = (4, 3, 5, 2, 6, 1, 7, 0)
VMEM = 16 * 1024 * 1024


def dft_tables():
    indices = np.arange(PW, dtype=np.int64)
    phases = (indices[:, None] * indices[None, :] % PW).astype(np.float64) * (2.0 * math.pi / PW)
    factor = 1.0 / math.sqrt(PW)
    re = (np.cos(phases) * factor).astype(ml_dtypes.bfloat16)
    im = (-np.sin(phases) * factor).astype(ml_dtypes.bfloat16)
    forward = np.block([[re, im], [-im, re]])
    inverse = np.block([[re, -im], [im, re]])
    return forward.astype(ml_dtypes.bfloat16), inverse.astype(ml_dtypes.bfloat16)


class Here:
    def __init__(self):
        s = lax.axis_index("slab")
        a = lax.axis_index("angle")
        self.a = a
        self.c = lax.rem(s, 2)
        self.xl = lax.rem(lax.div(s, 2), 2)
        self.zc = lax.div(s, 4)
        self.y = lax.rem(a, NY)
        self.xh = lax.div(a, NY)
        self.m = self.xl * NZC + self.zc

    def z_of(self, rel):
        return lax.rem(self.zc + rel, NZC)

    def y_of(self, rel):
        return lax.rem(self.y + rel, NY)

    def x_of(self, flip):
        return 1 - self.xl if flip else self.xl

    def chip(self, rel_z, flip_x):
        return self.device(zc=self.z_of(rel_z), xl=self.x_of(flip_x))

    def angle_peer(self, flip_xh, rel_y):
        return self.device(xh=1 - self.xh if flip_xh else self.xh, y=self.y_of(rel_y))

    def device(self, zc=None, xl=None, c=None, xh=None, y=None):
        zc = self.zc if zc is None else zc
        xl = self.xl if xl is None else xl
        c = self.c if c is None else c
        xh = self.xh if xh is None else xh
        y = self.y if y is None else y
        return {"slab": zc * 4 + xl * 2 + c, "angle": xh * NY + y}

    @property
    def sibling(self):
        return self.device(c=1 - self.c)

    def greet(self):
        peers = [self.chip(r, f) for r in FAR_FIRST for f in (1, 0) if r or f]
        peers[8:8] = [self.angle_peer(f, r) for f in (1, 0) for r in (2, 1, 3, 0) if r or f]
        peers.append(self.sibling)
        barrier = pltpu.get_barrier_semaphore()
        for peer in peers:
            pl.semaphore_signal(barrier, 1, device_id=peer, device_id_type=pl.DeviceIdType.MESH)
        pl.semaphore_wait(barrier, len(peers))


def rows16(block):
    return pl.ds(pl.multiple_of(block * BLOCK, BLOCK), BLOCK)


def half_cols(core):
    return pl.ds(pl.multiple_of(core * HALF, HALF), HALF)


def chunk_cols(y):
    return pl.ds(pl.multiple_of(y * CHUNK, CHUNK), CHUNK)


def remote(src, dst, send, recv, to):
    return pltpu.make_async_remote_copy(
        src_ref=src,
        dst_ref=dst,
        send_sem=send,
        recv_sem=recv,
        device_id=to,
        device_id_type=pl.DeviceIdType.MESH,
    )


def shifted_tiles(tiles, start, count):
    first = start >> 7
    inner = start & (LANES - 1)
    need = min(count + 1, TILES)
    for level in (3, 2, 1, 0):
        stride = 1 << level
        keep = min(need + stride - 1, TILES)
        bit = (first >> level) & 1 == 1
        size = len(tiles)
        tiles = [lax.select_n(bit, tiles[j], tiles[(j + stride) % size]) for j in range(keep)]
    back = (LANES - inner) & (LANES - 1)
    lane = lax.broadcasted_iota(jnp.int32, tiles[0].shape, 1)
    stay = lane < LANES - inner
    turned = [pltpu.roll(tile.astype(jnp.float32), back, 1) for tile in tiles]
    return [jnp.where(stay, turned[j], turned[(j + 1) % need]) for j in range(count)]


def tiles_of(row):
    return [row[:, j * LANES : (j + 1) * LANES] for j in range(TILES)]


class Copies:
    def __init__(self, here):
        self.here = here
        self.sent = []

    def start(self, src, dst, send, recv, to):
        copy = remote(src, dst, send, recv, to)
        copy.start()
        self.sent.append(copy)

    def arrived(self, ref, recv):
        remote(ref, ref, recv, recv, self.here.sibling).wait_recv()

    def drain(self):
        for copy in self.sent:
            copy.wait_send()


WHOLE = ((1, 0), (0, 7), (0, 1))
PIECES = ((7, (1,)), (1, (1,)), (2, (0, 1)), (6, (0, 1)), (3, (0, 1)), (5, (0, 1)), (4, (0, 1)))


def to_y(here, copies, piece, k, sems):
    send, recv = sems
    mine = piece(here.y)
    for d in (2, 1, 3):
        copies.start(mine, mine, send.at[d, k], recv.at[NY - d, k], here.angle_peer(0, d))


def from_y(here, copies, piece, k, sems):
    send, recv = sems
    for d in (1, 3, 2):
        copies.arrived(piece(here.y_of(d)), recv.at[d, k])


def project_kernel(
    vol, off, proj, offs_out, gath, acc, sib, offt, offv, off_s, offs_s,
    s_off, r_off, s_t1, r_t1, s_y, r_y, s_sib, r_sib, s_z, r_z, s_x, r_x, s_c, r_c, s_oa, r_oa, l_sem,
):
    here = Here()
    fetch = pltpu.make_async_copy(off, off_s, l_sem.at[2])
    fetch.start()
    here.greet()
    copies = Copies(here)
    order = (0, 1, 7, 2, 6, 3, 5, 4)
    cols = chunk_cols(here.y)

    def send_block(f, rel, where):
        r = (NZC - rel) % NZC
        to = here.chip(r, f)
        block = here.x_of(f) * NZC + here.z_of(r)
        copies.start(vol.at[rows16(block), where], gath.at[f, rel, :, where], s_t1.at[f, rel], r_t1.at[f, rel], to)

    for rel, flips in PIECES:
        for f in flips:
            send_block(f, rel, cols)
    for f, rel in WHOLE:
        send_block(f, rel, slice(None))
    own = pltpu.make_async_copy(vol.at[rows16(here.m)], gath.at[0, 0], l_sem.at[0])
    own.start()
    fetch.wait()
    offt[here.m] = jnp.full((1, LANES), off_s[0, 0], jnp.int32)
    for rel in order:
        for f in (0, 1):
            if rel or f:
                to = here.chip((NZC - rel) % NZC, f)
                copies.start(offt.at[here.m], offt.at[here.m], s_off.at[f, rel], r_off.at[f, rel], to)

    def piece(rel, flips):
        f = slice(None) if len(flips) == 2 else flips[0]
        return lambda y: gath.at[f, rel, :, chunk_cols(y)]

    for rel, flips in PIECES:
        for f in flips:
            copies.arrived(gath.at[f, rel, :, cols], r_t1.at[f, rel])
        to_y(here, copies, piece(rel, flips), rel, (s_y, r_y))

    for f in (0, 1):
        for r in range(NZC):
            if r or f:
                copies.arrived(offt.at[here.x_of(f) * NZC + here.z_of(r)], r_off.at[f, r])
    lane = lax.broadcasted_iota(jnp.int32, (1, LANES), 1)
    packed = jnp.zeros((1, LANES), jnp.int32)
    for g in range(NXL * NZC):
        packed = jnp.where(lane == g, offt[g], packed)
    offv[...] = packed
    down = pltpu.make_async_copy(offv, offs_s, l_sem.at[1])
    down.start()
    for f in (0, 1):
        for r in range(NY):
            if r or f:
                back = (NY - r) % NY
                copies.start(offv, offs_out.at[here.a], s_oa.at[f, r], r_oa.at[f, back], here.angle_peer(f, r))
    offs_out[here.a] = packed
    down.wait()
    own.wait()
    acc[...] = jnp.zeros_like(acc)

    def add_slot(f, rel):
        g = lax.rem(here.xl + f, NXL) * NZC + here.z_of(rel)
        for j, tile in enumerate(shifted_tiles(tiles_of(gath[f, rel]), offs_s[0, g], TILES)):
            acc[:, j * LANES : (j + 1) * LANES] += tile

    add_slot(0, 0)
    for f, rel in WHOLE:
        copies.arrived(gath.at[f, rel], r_t1.at[f, rel])
        add_slot(f, rel)
    for rel, flips in PIECES:
        from_y(here, copies, piece(rel, flips), rel, (s_y, r_y))
        for f in flips:
            add_slot(f, rel)

    mine, other = half_cols(here.c), half_cols(1 - here.c)
    copies.start(acc.at[:, other], sib, s_sib, r_sib, here.sibling)
    copies.arrived(sib, r_sib)
    proj[rows16(here.m), mine] = (acc[:, mine] + sib[...]).astype(jnp.bfloat16)

    own = proj.at[rows16(here.m), mine]
    for r in (1, 7, 2, 6, 3, 5, 4):
        copies.start(own, own, s_z.at[r], r_z.at[(NZC - r) % NZC], here.chip(r, 0))
    copies.start(own, own, s_x.at[0], r_x.at[0], here.chip(0, 1))
    copies.start(own, own, s_c.at[0, 0], r_c.at[0, 0], here.sibling)
    for rel in (1, 7, 2, 6, 3, 5, 4):
        got = proj.at[rows16(here.xl * NZC + here.z_of(rel)), mine]
        copies.arrived(got, r_z.at[rel])
        copies.start(got, got, s_x.at[rel], r_x.at[rel], here.chip(0, 1))
        copies.start(got, got, s_c.at[0, rel], r_c.at[0, rel], here.sibling)
    for rel in order:
        got = proj.at[rows16(here.x_of(1) * NZC + here.z_of(rel)), mine]
        copies.arrived(got, r_x.at[rel])
        copies.start(got, got, s_c.at[1, rel], r_c.at[1, rel], here.sibling)
    for f in (0, 1):
        for rel in order:
            copies.arrived(proj.at[rows16(here.x_of(f) * NZC + here.z_of(rel)), other], r_c.at[f, rel])
    for f in (0, 1):
        for r in range(NY):
            if r or f:
                a_from = (1 - here.xh if f else here.xh) * NY + here.y_of(r)
                copies.arrived(offs_out.at[a_from], r_oa.at[f, r])
    copies.drain()


GROUP = 16
BATCHES = 2
LINES = BLOCK // BATCHES
PACK = HALF // 2
QUARTER = CHUNK // 2


def pack(x):
    n = x.shape[1] // 2
    return jnp.concatenate([x[:, :n], x[:, n:]], axis=0)


def unpack(x):
    return jnp.concatenate([x[:LINES], x[LINES:]], axis=1)


def wave_kernel(proj, probe, measured, pos, forward, inverse, out, total):
    total[...] = jnp.zeros_like(total)
    count = measured.shape[1] // PW

    def swap(x):
        n = x.shape[0] // PW
        parts = [[x[k * PW : (k + 1) * PW, h * PW : (h + 1) * PW] for k in range(n)] for h in range(2)]
        return jnp.concatenate([jnp.concatenate(p, axis=1) for p in parts], axis=0)

    def one_group(group, carry):
        p_re = probe[0].astype(jnp.float32)
        p_im = probe[1].astype(jnp.float32)
        fwd = forward[...]
        inv = inverse[...]
        starts = []
        exits = []
        for k in range(GROUP):
            at = pos[GROUP * group + k]
            first = jnp.minimum(lax.div(at, LANES), TILES - 2)
            inner = at - first * LANES
            where = pl.ds(pl.multiple_of(first * LANES, LANES), 2 * LANES)
            starts.append((where, inner))
            row = lax.broadcasted_iota(jnp.int32, (2 * LANES, PW), 0)
            col = lax.broadcasted_iota(jnp.int32, (2 * LANES, PW), 1)
            pick = jnp.where(row == col + inner, 1.0, 0.0).astype(jnp.bfloat16)
            patch = jnp.dot(proj[:, where], pick, preferred_element_type=jnp.float32)
            re, im = patch[:PW], patch[PW:]
            exits.append(
                jnp.concatenate([p_re * re - p_im * im, p_re * im + p_im * re], axis=1).astype(jnp.bfloat16)
            )
        half = jnp.dot(jnp.concatenate(exits, axis=0), fwd, preferred_element_type=jnp.float32).astype(jnp.bfloat16)
        far = jnp.dot(inv, swap(half), preferred_element_type=jnp.float32)
        waves = []
        for k in range(GROUP):
            f_re = far[:PW, k * PW : (k + 1) * PW]
            f_im = far[PW:, k * PW : (k + 1) * PW]
            at = pl.multiple_of((GROUP * group + k) * PW, PW)
            target = measured[:, pl.ds(at, PW)].astype(jnp.float32)
            misfit = f_re * f_re + f_im * f_im - target
            waves.append(jnp.concatenate([misfit * f_re, misfit * f_im], axis=1).astype(jnp.bfloat16))
        back = jnp.dot(jnp.concatenate(waves, axis=0), inv, preferred_element_type=jnp.float32).astype(jnp.bfloat16)
        grad = jnp.dot(fwd, swap(back), preferred_element_type=jnp.float32)
        placed = []
        for k, (where, inner) in enumerate(starts):
            g_re = grad[:PW, k * PW : (k + 1) * PW]
            g_im = grad[PW:, k * PW : (k + 1) * PW]
            patch_grad = jnp.concatenate(
                [p_re * g_re + p_im * g_im, p_re * g_im - p_im * g_re], axis=0
            ).astype(jnp.bfloat16)
            row = lax.broadcasted_iota(jnp.int32, (PW, 2 * LANES), 0)
            col = lax.broadcasted_iota(jnp.int32, (PW, 2 * LANES), 1)
            put = jnp.where(col == row + inner, 1.0, 0.0).astype(jnp.bfloat16)
            placed.append(jnp.dot(patch_grad, put, preferred_element_type=jnp.float32))
        for (where, inner), value in zip(starts, placed):
            total[:, where] += value
        return carry

    lax.fori_loop(0, count // GROUP, one_group, 0)
    for m in range(NXL * NZC):
        for h in range(BATCHES):
            for c in range(2):
                x = total[m * BLOCK + h * LINES : m * BLOCK + (h + 1) * LINES, c * HALF : (c + 1) * HALF]
                out[h, c, m] = pack(x).astype(jnp.bfloat16)


def volume_kernel(
    part, offs, out, cbuf, xsend, xbuf, zsend, zbuf, dgall, vsend,
    s_c, r_c, s_x, r_x, s_z, r_z, s_a, r_a, s_s, r_s, s_v, r_v, s_y, r_y,
):
    here = Here()
    here.greet()
    copies = Copies(here)
    f32 = jnp.float32
    batches = range(BATCHES)

    def block(f, r):
        return here.x_of(f) * NZC + here.z_of(r)

    for h in batches:
        for f in (1, 0):
            for r in FAR_FIRST:
                copies.start(
                    part.at[h, 1 - here.c, block(f, r)], cbuf.at[h, f, r], s_c.at[h, f, r], r_c.at[h, f, r], here.sibling
                )
    for h in batches:
        for r in FAR_FIRST:
            copies.arrived(cbuf.at[h, 1, r], r_c.at[h, 1, r])
            value = part[h, here.c, block(1, r)].astype(f32) + cbuf[h, 1, r].astype(f32)
            xsend[h, r] = value.astype(jnp.bfloat16)
            copies.start(xsend.at[h, r], xbuf.at[h, r], s_x.at[h, r], r_x.at[h, r], here.chip(0, 1))
    totals = []
    for h in batches:
        for r in FAR_FIRST:
            copies.arrived(cbuf.at[h, 0, r], r_c.at[h, 0, r])
            value = part[h, here.c, block(0, r)].astype(f32) + cbuf[h, 0, r].astype(f32)
            copies.arrived(xbuf.at[h, r], r_x.at[h, r])
            value = value + xbuf[h, r].astype(f32)
            if r:
                zsend[h, r] = value.astype(jnp.bfloat16)
                slot = (NZC - r) % NZC
                copies.start(zsend.at[h, r], zbuf.at[h, slot], s_z.at[h, r], r_z.at[h, slot], here.chip(r, 0))
            else:
                totals.append(value)
    peers = [(0, 1), (0, 3), (1, 0), (0, 2), (1, 1), (1, 3), (1, 2)]
    for h in batches:
        total = totals[h]
        for r in (1, 7, 2, 6, 3, 5, 4):
            copies.arrived(zbuf.at[h, r], r_z.at[h, r])
            total = total + zbuf[h, r].astype(f32)
        dgall[h, here.a, here.c] = total.astype(jnp.bfloat16)
        own = dgall.at[h, here.a, here.c]
        for f, r in peers:
            copies.start(own, own, s_a.at[h, f, r], r_a.at[h, f, (NY - r) % NY], here.angle_peer(f, r))
        copies.start(own, own, s_s.at[h, 0, 0], r_s.at[h, 0, 0], here.sibling)

    def angle_of(f, r):
        return (1 - here.xh if f else here.xh) * NY + here.y_of(r)

    def gradient(h, f, rel, start, count):
        g = here.x_of(f) * NZC + here.z_of((NZC - rel) % NZC)
        sums = None
        for b in range(ANGLES):
            first = (start + NX - offs[b, g]) & (NX - 1)
            tiles = []
            for c in range(2):
                row = unpack(dgall[h, b, c].astype(f32))
                tiles += [row[:, j * LANES : (j + 1) * LANES] for j in range(TILES // 2)]
            tiles = shifted_tiles(tiles, first, count)
            sums = tiles if sums is None else [x + t for x, t in zip(sums, tiles)]
        return sums

    def quarter(sums):
        return pack(jnp.concatenate(sums, axis=1)).astype(jnp.bfloat16)

    per = CHUNK // LANES

    def send_block(h, f, rel, src, dst):
        copies.start(src, dst, s_v.at[h, f, rel], r_v.at[h, f, rel], here.chip((NZC - rel) % NZC, f))

    for h in batches:
        for f, r in peers:
            got = dgall.at[h, angle_of(f, r), here.c]
            copies.arrived(got, r_a.at[h, f, r])
            copies.start(got, got, s_s.at[h, f, r], r_s.at[h, f, r], here.sibling)
        for f, r in [(0, 0)] + peers:
            copies.arrived(dgall.at[h, angle_of(f, r), 1 - here.c], r_s.at[h, f, r])
        for rel, flips in PIECES:
            for f in flips:
                vsend[h, f, rel, here.y] = quarter(gradient(h, f, rel, here.y * CHUNK, per))
                send_block(h, f, rel, vsend.at[h, f, rel, here.y], out.at[here.xl, here.zc, h, here.y])
        for f, rel in WHOLE:
            sums = gradient(h, f, rel, 0, TILES)
            for y in range(NY):
                vsend[h, f, rel, y] = quarter(sums[y * per : (y + 1) * per])
            send_block(h, f, rel, vsend.at[h, f, rel], out.at[here.xl, here.zc, h])
        sums = gradient(h, 0, 0, 0, TILES)
        for y in range(NY):
            out[here.xl, here.zc, h, y] = quarter(sums[y * per : (y + 1) * per])

    def piece(h, rel, flips):
        f = slice(None) if len(flips) == 2 else here.x_of(flips[0])
        return lambda y: out.at[f, here.z_of(rel), h, y]

    for h in batches:
        for rel, flips in PIECES:
            for f in flips:
                copies.arrived(out.at[here.x_of(f), here.z_of(rel), h, here.y], r_v.at[h, f, rel])
            to_y(here, copies, piece(h, rel, flips), rel, (s_y.at[h], r_y.at[h]))
    for h in batches:
        for f, rel in WHOLE:
            copies.arrived(out.at[here.x_of(f), here.z_of(rel), h], r_v.at[h, f, rel])
        for rel, flips in PIECES:
            from_y(here, copies, piece(h, rel, flips), rel, (s_y.at[h], r_y.at[h]))
    copies.drain()


def update_kernel(rate, grad, volume, consensus, out, made, sems):
    copies = []
    for m in range(NXL * NZC):
        rows = slice(m * BLOCK, (m + 1) * BLOCK)
        current = volume[rows].astype(jnp.float32)
        kept = current - MIX * (current - consensus[rows].astype(jnp.float32))
        for h in range(BATCHES):
            for y in range(NY):
                step = unpack(grad[m, h, y].astype(jnp.float32))
                lines = slice(h * LINES, (h + 1) * LINES)
                cols = slice(y * CHUNK, (y + 1) * CHUNK)
                made[m * BLOCK + h * LINES : m * BLOCK + (h + 1) * LINES, cols] = kept[lines, cols] - rate * step
        copies.append(pltpu.make_async_copy(made.at[rows], out.at[rows], sems.at[m]))
        copies[-1].start()
    for copy in copies:
        copy.wait()


def dma(*shape):
    return pltpu.SemaphoreType.DMA(shape)


def vmem():
    return pl.BlockSpec(memory_space=pltpu.VMEM)


def smem():
    return pl.BlockSpec(memory_space=pltpu.SMEM)


def project(lines, off):
    return pl.pallas_call(
        project_kernel,
        out_shape=(
            jax.ShapeDtypeStruct((2 * PW, NX), jnp.bfloat16),
            jax.ShapeDtypeStruct((ANGLES, 1, LANES), jnp.int32),
        ),
        in_specs=[pl.BlockSpec(memory_space=pl.ANY), pl.BlockSpec(memory_space=pl.ANY)],
        out_specs=(vmem(), vmem()),
        scratch_shapes=[
            pltpu.VMEM((NXL, NZC, BLOCK, NX), jnp.bfloat16),
            pltpu.VMEM((BLOCK, NX), jnp.float32),
            pltpu.VMEM((BLOCK, HALF), jnp.float32),
            pltpu.VMEM((NXL * NZC, 1, LANES), jnp.int32),
            pltpu.VMEM((1, LANES), jnp.int32),
            pltpu.SMEM((1, 1), jnp.int32),
            pltpu.SMEM((1, LANES), jnp.int32),
            dma(NXL, NZC), dma(NXL, NZC), dma(NXL, NZC), dma(NXL, NZC),
            dma(NY, NZC), dma(NY, NZC),
            pltpu.SemaphoreType.DMA, pltpu.SemaphoreType.DMA,
            dma(NZC), dma(NZC), dma(NZC), dma(NZC),
            dma(NXL, NZC), dma(NXL, NZC),
            dma(NXH, NY), dma(NXH, NY),
            dma(3),
        ],
        compiler_params=pltpu.CompilerParams(collective_id=0, has_side_effects=True, vmem_limit_bytes=52 * 1024 * 1024),
        name="project",
    )(lines, off)


def waves(proj, probe, measured, pos, forward, inverse):
    return pl.pallas_call(
        wave_kernel,
        out_shape=jax.ShapeDtypeStruct((BATCHES, 2, NXL * NZC, BLOCK, PACK), jnp.bfloat16),
        in_specs=[vmem(), vmem(), vmem(), smem(), vmem(), vmem()],
        out_specs=vmem(),
        scratch_shapes=[pltpu.VMEM((2 * PW, NX), jnp.float32)],
        compiler_params=pltpu.CompilerParams(vmem_limit_bytes=2 * VMEM),
        name="waves",
    )(proj, probe, measured, pos, forward, inverse)


def volume_gradient(part, offs):
    bf16 = jnp.bfloat16
    small = (BATCHES, NZC, BLOCK, PACK)
    return pl.pallas_call(
        volume_kernel,
        out_shape=jax.ShapeDtypeStruct((NXL, NZC, BATCHES, NY, BLOCK, QUARTER), bf16),
        in_specs=[vmem(), smem()],
        out_specs=vmem(),
        scratch_shapes=[
            pltpu.VMEM((BATCHES, NXL, NZC, BLOCK, PACK), bf16),
            pltpu.VMEM(small, bf16),
            pltpu.VMEM(small, bf16),
            pltpu.VMEM(small, bf16),
            pltpu.VMEM(small, bf16),
            pltpu.VMEM((BATCHES, ANGLES, 2, BLOCK, PACK), bf16),
            pltpu.VMEM((BATCHES, NXL, NZC, NY, BLOCK, QUARTER), bf16),
            dma(BATCHES, NXL, NZC), dma(BATCHES, NXL, NZC),
            dma(BATCHES, NZC), dma(BATCHES, NZC), dma(BATCHES, NZC), dma(BATCHES, NZC),
            dma(BATCHES, NXH, NY), dma(BATCHES, NXH, NY), dma(BATCHES, NXH, NY), dma(BATCHES, NXH, NY),
            dma(BATCHES, NXL, NZC), dma(BATCHES, NXL, NZC),
            dma(BATCHES, NY, NZC), dma(BATCHES, NY, NZC),
        ],
        compiler_params=pltpu.CompilerParams(collective_id=1, has_side_effects=True, vmem_limit_bytes=VMEM),
        cost_estimate=pl.CostEstimate(flops=10**8, bytes_accessed=10**8, transcendentals=0),
        name="volume_gradient",
    )(part, offs)


def update(rate, grad, lines, consensus):
    return pl.pallas_call(
        functools.partial(update_kernel, rate),
        out_shape=jax.ShapeDtypeStruct((2 * PW, NX), jnp.float32),
        in_specs=[vmem(), vmem(), vmem()],
        out_specs=pl.BlockSpec(memory_space=pl.ANY),
        scratch_shapes=[pltpu.VMEM((2 * PW, NX), jnp.float32), dma(NXL * NZC)],
        compiler_params=pltpu.CompilerParams(vmem_limit_bytes=VMEM),
        name="update",
    )(grad, lines, consensus)


def per_device(volume, consensus, probe, intensities, positions, offsets):
    pos_count = positions.shape[1]
    forward, inverse = dft_tables()
    lines = volume.reshape(2 * PW, NX)
    measured = intensities.reshape(PW, pos_count * PW)
    proj, offs = project(lines, offsets)
    part = waves(proj, probe, measured, positions.reshape(-1), jnp.asarray(forward), jnp.asarray(inverse))
    grad = volume_gradient(part, offs.reshape(ANGLES, LANES))
    rate = math.sqrt(NX / (pos_count * lax.axis_size("slab") * ANGLES * PW))
    grad = grad.reshape(NXL * NZC, BATCHES, NY, BLOCK, QUARTER)
    return update(rate, grad, lines, consensus.reshape(2 * PW, NX)).reshape(volume.shape)


def solution(mesh):
    return jax.shard_map(
        per_device,
        mesh=mesh,
        in_specs=(
            P(None, "slab", None, None),
            P(None, "slab", None, None),
            P(),
            P("angle", None, "slab", None),
            P("angle", "slab"),
            P("angle", "slab"),
        ),
        out_specs=P(None, "slab", None, None),
        check_vma=False,
    )
```

```python
import functools
import math

import jax
import jax.numpy as jnp
import ml_dtypes
import numpy as np
from jax import lax
from jax.experimental import pallas as pl
from jax.experimental.pallas import tpu as pltpu
from jax.sharding import PartitionSpec as P

MIX = 0.5
NX = 2048
PW = 128
LANES = 128
TILES = NX // LANES
NZC = 8
NXL = 2
NXH = 2
NY = 4
ANGLES = NXH * NY
BLOCK = 16
HALF = NX // 2
CHUNK = NX // NY
FAR_FIRST = (4, 3, 5, 2, 6, 1, 7, 0)
VMEM = 16 * 1024 * 1024


def dft_tables():
    indices = np.arange(PW, dtype=np.int64)
    phases = (indices[:, None] * indices[None, :] % PW).astype(np.float64) * (2.0 * math.pi / PW)
    factor = 1.0 / math.sqrt(PW)
    re = (np.cos(phases) * factor).astype(ml_dtypes.bfloat16)
    im = (-np.sin(phases) * factor).astype(ml_dtypes.bfloat16)
    forward = np.block([[re, im], [-im, re]])
    inverse = np.block([[re, -im], [im, re]])
    return forward.astype(ml_dtypes.bfloat16), inverse.astype(ml_dtypes.bfloat16)


class Here:
    def __init__(self):
        s = lax.axis_index("slab")
        a = lax.axis_index("angle")
        self.a = a
        self.c = lax.rem(s, 2)
        self.xl = lax.rem(lax.div(s, 2), 2)
        self.zc = lax.div(s, 4)
        self.y = lax.rem(a, NY)
        self.xh = lax.div(a, NY)
        self.m = self.xl * NZC + self.zc

    def z_of(self, rel):
        return lax.rem(self.zc + rel, NZC)

    def y_of(self, rel):
        return lax.rem(self.y + rel, NY)

    def x_of(self, flip):
        return 1 - self.xl if flip else self.xl

    def chip(self, rel_z, flip_x):
        return self.device(zc=self.z_of(rel_z), xl=self.x_of(flip_x))

    def angle_peer(self, flip_xh, rel_y):
        return self.device(xh=1 - self.xh if flip_xh else self.xh, y=self.y_of(rel_y))

    def device(self, zc=None, xl=None, c=None, xh=None, y=None):
        zc = self.zc if zc is None else zc
        xl = self.xl if xl is None else xl
        c = self.c if c is None else c
        xh = self.xh if xh is None else xh
        y = self.y if y is None else y
        return {"slab": zc * 4 + xl * 2 + c, "angle": xh * NY + y}

    @property
    def sibling(self):
        return self.device(c=1 - self.c)

    def greet(self):
        peers = [self.chip(r, f) for r in FAR_FIRST for f in (1, 0) if r or f]
        peers[8:8] = [self.angle_peer(f, r) for f in (1, 0) for r in (2, 1, 3, 0) if r or f]
        peers.append(self.sibling)
        barrier = pltpu.get_barrier_semaphore()
        for peer in peers:
            pl.semaphore_signal(barrier, 1, device_id=peer, device_id_type=pl.DeviceIdType.MESH)
        pl.semaphore_wait(barrier, len(peers))


def rows16(block):
    return pl.ds(pl.multiple_of(block * BLOCK, BLOCK), BLOCK)


def half_cols(core):
    return pl.ds(pl.multiple_of(core * HALF, HALF), HALF)


def chunk_cols(y):
    return pl.ds(pl.multiple_of(y * CHUNK, CHUNK), CHUNK)


def remote(src, dst, send, recv, to):
    return pltpu.make_async_remote_copy(
        src_ref=src,
        dst_ref=dst,
        send_sem=send,
        recv_sem=recv,
        device_id=to,
        device_id_type=pl.DeviceIdType.MESH,
    )


def shifted_tiles(tiles, start, count):
    first = start >> 7
    inner = start & (LANES - 1)
    need = min(count + 1, TILES)
    for level in (3, 2, 1, 0):
        stride = 1 << level
        keep = min(need + stride - 1, TILES)
        bit = (first >> level) & 1 == 1
        size = len(tiles)
        tiles = [lax.select_n(bit, tiles[j], tiles[(j + stride) % size]) for j in range(keep)]
    back = (LANES - inner) & (LANES - 1)
    lane = lax.broadcasted_iota(jnp.int32, tiles[0].shape, 1)
    stay = lane < LANES - inner
    turned = [pltpu.roll(tile.astype(jnp.float32), back, 1) for tile in tiles]
    return [jnp.where(stay, turned[j], turned[(j + 1) % need]) for j in range(count)]


def tiles_of(row):
    return [row[:, j * LANES : (j + 1) * LANES] for j in range(TILES)]


class Copies:
    def __init__(self, here):
        self.here = here
        self.sent = []

    def start(self, src, dst, send, recv, to):
        copy = remote(src, dst, send, recv, to)
        copy.start()
        self.sent.append(copy)

    def arrived(self, ref, recv):
        remote(ref, ref, recv, recv, self.here.sibling).wait_recv()

    def drain(self):
        for copy in self.sent:
            copy.wait_send()


WHOLE = ((1, 0), (0, 7), (0, 1), (1, 7), (1, 1))
PIECES = ((2, (0, 1)), (6, (0, 1)), (3, (0, 1)), (5, (0, 1)), (4, (0, 1)))
FWD = (0,)


def to_y(here, copies, piece, k, sems):
    send, recv = sems
    mine = piece(here.y)
    for d in (2, 1, 3):
        copies.start(mine, mine, send.at[d, k], recv.at[NY - d, k], here.angle_peer(0, d))


def from_y(here, copies, piece, k, sems):
    send, recv = sems
    for d in (1, 3, 2):
        copies.arrived(piece(here.y_of(d)), recv.at[d, k])


def project_kernel(
    vol, off, proj, offs_out, gath, acc, sib, offt, offv, off_s, offs_s,
    s_off, r_off, s_t1, r_t1, s_y, r_y, s_sib, r_sib, s_z, r_z, s_x, r_x, s_c, r_c, s_oa, r_oa, l_sem,
):
    here = Here()
    fetch = pltpu.make_async_copy(off, off_s, l_sem.at[2])
    fetch.start()
    here.greet()
    copies = Copies(here)
    order = (0, 1, 7, 2, 6, 3, 5, 4)
    cols = chunk_cols(here.y)

    def send_block(f, rel, where):
        r = (NZC - rel) % NZC
        to = here.chip(r, f)
        block = here.x_of(f) * NZC + here.z_of(r)
        copies.start(vol.at[rows16(block), where], gath.at[f, rel, :, where], s_t1.at[f, rel], r_t1.at[f, rel], to)

    for rel, flips in PIECES:
        for f in flips:
            send_block(f, rel, cols)
    for f, rel in WHOLE:
        send_block(f, rel, slice(None))
    own = pltpu.make_async_copy(vol.at[rows16(here.m)], gath.at[0, 0], l_sem.at[0])
    own.start()
    fetch.wait()
    offt[here.m] = jnp.full((1, LANES), off_s[0, 0], jnp.int32)
    for rel in order:
        for f in (0, 1):
            if rel or f:
                to = here.chip((NZC - rel) % NZC, f)
                copies.start(offt.at[here.m], offt.at[here.m], s_off.at[f, rel], r_off.at[f, rel], to)

    def piece(rel, flips):
        f = slice(None) if len(flips) == 2 else flips[0]
        return lambda y: gath.at[f, rel, :, chunk_cols(y)]

    for rel, flips in PIECES:
        for f in flips:
            copies.arrived(gath.at[f, rel, :, cols], r_t1.at[f, rel])
        to_y(here, copies, piece(rel, flips), rel, (s_y, r_y))

    for f in (0, 1):
        for r in range(NZC):
            if r or f:
                copies.arrived(offt.at[here.x_of(f) * NZC + here.z_of(r)], r_off.at[f, r])
    lane = lax.broadcasted_iota(jnp.int32, (1, LANES), 1)
    packed = jnp.zeros((1, LANES), jnp.int32)
    for g in range(NXL * NZC):
        packed = jnp.where(lane == g, offt[g], packed)
    offv[...] = packed
    down = pltpu.make_async_copy(offv, offs_s, l_sem.at[1])
    down.start()
    for f in (0, 1):
        for r in range(NY):
            if r or f:
                back = (NY - r) % NY
                copies.start(offv, offs_out.at[here.a], s_oa.at[f, r], r_oa.at[f, back], here.angle_peer(f, r))
    offs_out[here.a] = packed
    down.wait()
    own.wait()
    acc[...] = jnp.zeros_like(acc)

    def add_slot(f, rel):
        g = lax.rem(here.xl + f, NXL) * NZC + here.z_of(rel)
        for j, tile in enumerate(shifted_tiles(tiles_of(gath[f, rel]), offs_s[0, g], TILES)):
            acc[:, j * LANES : (j + 1) * LANES] += tile

    add_slot(0, 0)
    for f, rel in WHOLE:
        copies.arrived(gath.at[f, rel], r_t1.at[f, rel])
        add_slot(f, rel)
    for rel, flips in PIECES:
        from_y(here, copies, piece(rel, flips), rel, (s_y, r_y))
        for f in flips:
            add_slot(f, rel)

    mine, other = half_cols(here.c), half_cols(1 - here.c)
    copies.start(acc.at[:, other], sib, s_sib, r_sib, here.sibling)
    copies.arrived(sib, r_sib)
    proj[rows16(here.m), mine] = (acc[:, mine] + sib[...]).astype(jnp.bfloat16)

    own = proj.at[rows16(here.m), mine]
    for r in (1, 7, 2, 6, 3, 5, 4):
        copies.start(own, own, s_z.at[r], r_z.at[(NZC - r) % NZC], here.chip(r, 0))
    copies.start(own, own, s_x.at[0], r_x.at[0], here.chip(0, 1))
    copies.start(own, own, s_c.at[0, 0], r_c.at[0, 0], here.sibling)
    for rel in (1, 7, 2, 6, 3, 5, 4):
        got = proj.at[rows16(here.xl * NZC + here.z_of(rel)), mine]
        copies.arrived(got, r_z.at[rel])
        copies.start(got, got, s_x.at[rel], r_x.at[rel], here.chip(0, 1))
        copies.start(got, got, s_c.at[0, rel], r_c.at[0, rel], here.sibling)
    for rel in order:
        got = proj.at[rows16(here.x_of(1) * NZC + here.z_of(rel)), mine]
        copies.arrived(got, r_x.at[rel])
        copies.start(got, got, s_c.at[1, rel], r_c.at[1, rel], here.sibling)
    for f in (0, 1):
        for rel in order:
            copies.arrived(proj.at[rows16(here.x_of(f) * NZC + here.z_of(rel)), other], r_c.at[f, rel])
    for f in (0, 1):
        for r in range(NY):
            if r or f:
                a_from = (1 - here.xh if f else here.xh) * NY + here.y_of(r)
                copies.arrived(offs_out.at[a_from], r_oa.at[f, r])
    copies.drain()


GROUP = 16
BATCHES = 2
LINES = BLOCK // BATCHES
PACK = HALF // 2
QUARTER = CHUNK // 2


def pack(x):
    n = x.shape[1] // 2
    return jnp.concatenate([x[:, :n], x[:, n:]], axis=0)


def unpack(x):
    return jnp.concatenate([x[:LINES], x[LINES:]], axis=1)


def wave_kernel(proj, probe, measured, pos, forward, inverse, out, total):
    total[...] = jnp.zeros_like(total)
    count = measured.shape[1] // PW

    def swap(x):
        n = x.shape[0] // PW
        parts = [[x[k * PW : (k + 1) * PW, h * PW : (h + 1) * PW] for k in range(n)] for h in range(2)]
        return jnp.concatenate([jnp.concatenate(p, axis=1) for p in parts], axis=0)

    def one_group(group, carry):
        p_re = probe[0].astype(jnp.float32)
        p_im = probe[1].astype(jnp.float32)
        fwd = forward[...]
        inv = inverse[...]
        starts = []
        exits = []
        for k in range(GROUP):
            at = pos[GROUP * group + k]
            first = jnp.minimum(lax.div(at, LANES), TILES - 2)
            inner = at - first * LANES
            where = pl.ds(pl.multiple_of(first * LANES, LANES), 2 * LANES)
            starts.append((where, inner))
            row = lax.broadcasted_iota(jnp.int32, (2 * LANES, PW), 0)
            col = lax.broadcasted_iota(jnp.int32, (2 * LANES, PW), 1)
            pick = jnp.where(row == col + inner, 1.0, 0.0).astype(jnp.bfloat16)
            patch = jnp.dot(proj[:, where], pick, preferred_element_type=jnp.float32)
            re, im = patch[:PW], patch[PW:]
            exits.append(
                jnp.concatenate([p_re * re - p_im * im, p_re * im + p_im * re], axis=1).astype(jnp.bfloat16)
            )
        half = jnp.dot(jnp.concatenate(exits, axis=0), fwd, preferred_element_type=jnp.float32).astype(jnp.bfloat16)
        far = jnp.dot(inv, swap(half), preferred_element_type=jnp.float32)
        waves = []
        for k in range(GROUP):
            f_re = far[:PW, k * PW : (k + 1) * PW]
            f_im = far[PW:, k * PW : (k + 1) * PW]
            at = pl.multiple_of((GROUP * group + k) * PW, PW)
            target = measured[:, pl.ds(at, PW)].astype(jnp.float32)
            misfit = f_re * f_re + f_im * f_im - target
            waves.append(jnp.concatenate([misfit * f_re, misfit * f_im], axis=1).astype(jnp.bfloat16))
        back = jnp.dot(jnp.concatenate(waves, axis=0), inv, preferred_element_type=jnp.float32).astype(jnp.bfloat16)
        grad = jnp.dot(fwd, swap(back), preferred_element_type=jnp.float32)
        placed = []
        for k, (where, inner) in enumerate(starts):
            g_re = grad[:PW, k * PW : (k + 1) * PW]
            g_im = grad[PW:, k * PW : (k + 1) * PW]
            patch_grad = jnp.concatenate(
                [p_re * g_re + p_im * g_im, p_re * g_im - p_im * g_re], axis=0
            ).astype(jnp.bfloat16)
            row = lax.broadcasted_iota(jnp.int32, (PW, 2 * LANES), 0)
            col = lax.broadcasted_iota(jnp.int32, (PW, 2 * LANES), 1)
            put = jnp.where(col == row + inner, 1.0, 0.0).astype(jnp.bfloat16)
            placed.append(jnp.dot(patch_grad, put, preferred_element_type=jnp.float32))
        for (where, inner), value in zip(starts, placed):
            total[:, where] += value
        return carry

    lax.fori_loop(0, count // GROUP, one_group, 0)
    for m in range(NXL * NZC):
        for h in range(BATCHES):
            for c in range(2):
                x = total[m * BLOCK + h * LINES : m * BLOCK + (h + 1) * LINES, c * HALF : (c + 1) * HALF]
                out[h, c, m] = pack(x).astype(jnp.bfloat16)


def volume_kernel(
    part, offs, out, cbuf, xsend, xbuf, zsend, zbuf, dgall, vsend,
    s_c, r_c, s_x, r_x, s_z, r_z, s_a, r_a, s_s, r_s, s_v, r_v, s_y, r_y,
):
    here = Here()
    here.greet()
    copies = Copies(here)
    f32 = jnp.float32
    batches = range(BATCHES)

    def block(f, r):
        return here.x_of(f) * NZC + here.z_of(r)

    for h in batches:
        for f in (1, 0):
            for r in FAR_FIRST:
                copies.start(
                    part.at[h, 1 - here.c, block(f, r)], cbuf.at[h, f, r], s_c.at[h, f, r], r_c.at[h, f, r], here.sibling
                )
    for h in batches:
        for r in FAR_FIRST:
            copies.arrived(cbuf.at[h, 1, r], r_c.at[h, 1, r])
            value = part[h, here.c, block(1, r)].astype(f32) + cbuf[h, 1, r].astype(f32)
            xsend[h, r] = value.astype(jnp.bfloat16)
            copies.start(xsend.at[h, r], xbuf.at[h, r], s_x.at[h, r], r_x.at[h, r], here.chip(0, 1))
    totals = []
    for h in batches:
        for r in FAR_FIRST:
            copies.arrived(cbuf.at[h, 0, r], r_c.at[h, 0, r])
            value = part[h, here.c, block(0, r)].astype(f32) + cbuf[h, 0, r].astype(f32)
            copies.arrived(xbuf.at[h, r], r_x.at[h, r])
            value = value + xbuf[h, r].astype(f32)
            if r:
                zsend[h, r] = value.astype(jnp.bfloat16)
                slot = (NZC - r) % NZC
                copies.start(zsend.at[h, r], zbuf.at[h, slot], s_z.at[h, r], r_z.at[h, slot], here.chip(r, 0))
            else:
                totals.append(value)
    peers = [(0, 1), (0, 3), (1, 0), (0, 2), (1, 1), (1, 3), (1, 2)]
    for h in batches:
        total = totals[h]
        for r in (1, 7, 2, 6, 3, 5, 4):
            copies.arrived(zbuf.at[h, r], r_z.at[h, r])
            total = total + zbuf[h, r].astype(f32)
        dgall[h, here.a, here.c] = total.astype(jnp.bfloat16)
        own = dgall.at[h, here.a, here.c]
        for f, r in peers:
            copies.start(own, own, s_a.at[h, f, r], r_a.at[h, f, (NY - r) % NY], here.angle_peer(f, r))
        copies.start(own, own, s_s.at[h, 0, 0], r_s.at[h, 0, 0], here.sibling)

    def angle_of(f, r):
        return (1 - here.xh if f else here.xh) * NY + here.y_of(r)

    def gradient(h, f, rel, start, count):
        g = here.x_of(f) * NZC + here.z_of((NZC - rel) % NZC)
        sums = None
        for b in range(ANGLES):
            first = (start + NX - offs[b, g]) & (NX - 1)
            tiles = []
            for c in range(2):
                row = unpack(dgall[h, b, c].astype(f32))
                tiles += [row[:, j * LANES : (j + 1) * LANES] for j in range(TILES // 2)]
            tiles = shifted_tiles(tiles, first, count)
            sums = tiles if sums is None else [x + t for x, t in zip(sums, tiles)]
        return sums

    def quarter(sums):
        return pack(jnp.concatenate(sums, axis=1)).astype(jnp.bfloat16)

    per = CHUNK // LANES

    def send_block(h, f, rel, src, dst):
        copies.start(src, dst, s_v.at[h, f, rel], r_v.at[h, f, rel], here.chip((NZC - rel) % NZC, f))

    for h in batches:
        for f, r in peers:
            got = dgall.at[h, angle_of(f, r), here.c]
            copies.arrived(got, r_a.at[h, f, r])
            copies.start(got, got, s_s.at[h, f, r], r_s.at[h, f, r], here.sibling)
        for f, r in [(0, 0)] + peers:
            copies.arrived(dgall.at[h, angle_of(f, r), 1 - here.c], r_s.at[h, f, r])
        for rel, flips in PIECES:
            for f in flips:
                vsend[h, f, rel, here.y] = quarter(gradient(h, f, rel, here.y * CHUNK, per))
                send_block(h, f, rel, vsend.at[h, f, rel, here.y], out.at[here.xl, here.zc, h, here.y])
        for f, rel in WHOLE:
            sums = gradient(h, f, rel, 0, TILES)
            for y in range(NY):
                vsend[h, f, rel, y] = quarter(sums[y * per : (y + 1) * per])
            send_block(h, f, rel, vsend.at[h, f, rel], out.at[here.xl, here.zc, h])
        sums = gradient(h, 0, 0, 0, TILES)
        for y in range(NY):
            out[here.xl, here.zc, h, y] = quarter(sums[y * per : (y + 1) * per])

    def piece(h, rel, flips):
        f = slice(None) if len(flips) == 2 else here.x_of(flips[0])
        return lambda y: out.at[f, here.z_of(rel), h, y]

    up, dn = here.angle_peer(0, 1), here.angle_peer(0, NY - 1)
    for h in batches:
        for rel, flips in PIECES:
            for f in flips:
                copies.arrived(out.at[here.x_of(f), here.z_of(rel), h, here.y], r_v.at[h, f, rel])
            mine = piece(h, rel, flips)(here.y)
            for d in (1, 3) if h in FWD else (2, 1, 3):
                copies.start(mine, mine, s_y.at[h, d, rel], r_y.at[h, NY - d, rel], here.angle_peer(0, d))
    for h in FWD:
        for k, (rel, flips) in enumerate(PIECES):
            d, to = ((3, up), (1, dn))[k % 2]
            got = piece(h, rel, flips)(here.y_of(d))
            copies.arrived(got, r_y.at[h, d, rel])
            copies.start(got, got, s_y.at[h, 2, rel], r_y.at[h, 2, rel], to)
    for h in batches:
        for f, rel in WHOLE:
            copies.arrived(out.at[here.x_of(f), here.z_of(rel), h], r_v.at[h, f, rel])
        for k, (rel, flips) in enumerate(PIECES):
            for d in (((1, 2), (3, 2))[k % 2]) if h in FWD else (1, 3, 2):
                copies.arrived(piece(h, rel, flips)(here.y_of(d)), r_y.at[h, d, rel])
    copies.drain()


def update_kernel(rate, grad, volume, consensus, out, made, sems):
    copies = []
    for m in range(NXL * NZC):
        rows = slice(m * BLOCK, (m + 1) * BLOCK)
        current = volume[rows].astype(jnp.float32)
        kept = current - MIX * (current - consensus[rows].astype(jnp.float32))
        for h in range(BATCHES):
            for y in range(NY):
                step = unpack(grad[m, h, y].astype(jnp.float32))
                lines = slice(h * LINES, (h + 1) * LINES)
                cols = slice(y * CHUNK, (y + 1) * CHUNK)
                made[m * BLOCK + h * LINES : m * BLOCK + (h + 1) * LINES, cols] = kept[lines, cols] - rate * step
        copies.append(pltpu.make_async_copy(made.at[rows], out.at[rows], sems.at[m]))
        copies[-1].start()
    for copy in copies:
        copy.wait()


def dma(*shape):
    return pltpu.SemaphoreType.DMA(shape)


def vmem():
    return pl.BlockSpec(memory_space=pltpu.VMEM)


def smem():
    return pl.BlockSpec(memory_space=pltpu.SMEM)


def project(lines, off):
    return pl.pallas_call(
        project_kernel,
        out_shape=(
            jax.ShapeDtypeStruct((2 * PW, NX), jnp.bfloat16),
            jax.ShapeDtypeStruct((ANGLES, 1, LANES), jnp.int32),
        ),
        in_specs=[pl.BlockSpec(memory_space=pl.ANY), pl.BlockSpec(memory_space=pl.ANY)],
        out_specs=(vmem(), vmem()),
        scratch_shapes=[
            pltpu.VMEM((NXL, NZC, BLOCK, NX), jnp.bfloat16),
            pltpu.VMEM((BLOCK, NX), jnp.float32),
            pltpu.VMEM((BLOCK, HALF), jnp.float32),
            pltpu.VMEM((NXL * NZC, 1, LANES), jnp.int32),
            pltpu.VMEM((1, LANES), jnp.int32),
            pltpu.SMEM((1, 1), jnp.int32),
            pltpu.SMEM((1, LANES), jnp.int32),
            dma(NXL, NZC), dma(NXL, NZC), dma(NXL, NZC), dma(NXL, NZC),
            dma(NY, NZC), dma(NY, NZC),
            pltpu.SemaphoreType.DMA, pltpu.SemaphoreType.DMA,
            dma(NZC), dma(NZC), dma(NZC), dma(NZC),
            dma(NXL, NZC), dma(NXL, NZC),
            dma(NXH, NY), dma(NXH, NY),
            dma(3),
        ],
        compiler_params=pltpu.CompilerParams(collective_id=0, has_side_effects=True, vmem_limit_bytes=52 * 1024 * 1024),
        name="project",
    )(lines, off)


def waves(proj, probe, measured, pos, forward, inverse):
    return pl.pallas_call(
        wave_kernel,
        out_shape=jax.ShapeDtypeStruct((BATCHES, 2, NXL * NZC, BLOCK, PACK), jnp.bfloat16),
        in_specs=[vmem(), vmem(), vmem(), smem(), vmem(), vmem()],
        out_specs=vmem(),
        scratch_shapes=[pltpu.VMEM((2 * PW, NX), jnp.float32)],
        compiler_params=pltpu.CompilerParams(vmem_limit_bytes=2 * VMEM),
        name="waves",
    )(proj, probe, measured, pos, forward, inverse)


def volume_gradient(part, offs):
    bf16 = jnp.bfloat16
    small = (BATCHES, NZC, BLOCK, PACK)
    return pl.pallas_call(
        volume_kernel,
        out_shape=jax.ShapeDtypeStruct((NXL, NZC, BATCHES, NY, BLOCK, QUARTER), bf16),
        in_specs=[vmem(), smem()],
        out_specs=vmem(),
        scratch_shapes=[
            pltpu.VMEM((BATCHES, NXL, NZC, BLOCK, PACK), bf16),
            pltpu.VMEM(small, bf16),
            pltpu.VMEM(small, bf16),
            pltpu.VMEM(small, bf16),
            pltpu.VMEM(small, bf16),
            pltpu.VMEM((BATCHES, ANGLES, 2, BLOCK, PACK), bf16),
            pltpu.VMEM((BATCHES, NXL, NZC, NY, BLOCK, QUARTER), bf16),
            dma(BATCHES, NXL, NZC), dma(BATCHES, NXL, NZC),
            dma(BATCHES, NZC), dma(BATCHES, NZC), dma(BATCHES, NZC), dma(BATCHES, NZC),
            dma(BATCHES, NXH, NY), dma(BATCHES, NXH, NY), dma(BATCHES, NXH, NY), dma(BATCHES, NXH, NY),
            dma(BATCHES, NXL, NZC), dma(BATCHES, NXL, NZC),
            dma(BATCHES, NY, NZC), dma(BATCHES, NY, NZC),
        ],
        compiler_params=pltpu.CompilerParams(collective_id=1, has_side_effects=True, vmem_limit_bytes=VMEM),
        cost_estimate=pl.CostEstimate(flops=10**8, bytes_accessed=10**8, transcendentals=0),
        name="volume_gradient",
    )(part, offs)


def update(rate, grad, lines, consensus):
    return pl.pallas_call(
        functools.partial(update_kernel, rate),
        out_shape=jax.ShapeDtypeStruct((2 * PW, NX), jnp.float32),
        in_specs=[vmem(), vmem(), vmem()],
        out_specs=pl.BlockSpec(memory_space=pl.ANY),
        scratch_shapes=[pltpu.VMEM((2 * PW, NX), jnp.float32), dma(NXL * NZC)],
        compiler_params=pltpu.CompilerParams(vmem_limit_bytes=VMEM),
        name="update",
    )(grad, lines, consensus)


def per_device(volume, consensus, probe, intensities, positions, offsets):
    pos_count = positions.shape[1]
    forward, inverse = dft_tables()
    lines = volume.reshape(2 * PW, NX)
    measured = intensities.reshape(PW, pos_count * PW)
    proj, offs = project(lines, offsets)
    part = waves(proj, probe, measured, positions.reshape(-1), jnp.asarray(forward), jnp.asarray(inverse))
    grad = volume_gradient(part, offs.reshape(ANGLES, LANES))
    rate = math.sqrt(NX / (pos_count * lax.axis_size("slab") * ANGLES * PW))
    grad = grad.reshape(NXL * NZC, BATCHES, NY, BLOCK, QUARTER)
    return update(rate, grad, lines, consensus.reshape(2 * PW, NX)).reshape(volume.shape)


def solution(mesh):
    return jax.shard_map(
        per_device,
        mesh=mesh,
        in_specs=(
            P(None, "slab", None, None),
            P(None, "slab", None, None),
            P(),
            P("angle", None, "slab", None),
            P("angle", "slab"),
            P("angle", "slab"),
        ),
        out_specs=P(None, "slab", None, None),
        check_vma=False,
    )
```

```python
import functools
import math

import jax
import jax.numpy as jnp
import ml_dtypes
import numpy as np
from jax import lax
from jax.experimental import pallas as pl
from jax.experimental.pallas import tpu as pltpu
from jax.sharding import PartitionSpec as P

MIX = 0.5
NX = 2048
PW = 128
LANES = 128
TILES = NX // LANES
NZC = 8
NXL = 2
NXH = 2
NY = 4
ANGLES = NXH * NY
BLOCK = 16
HALF = NX // 2
CHUNK = NX // NY
FAR_FIRST = (4, 3, 5, 2, 6, 1, 7, 0)
VMEM = 16 * 1024 * 1024


def dft_tables():
    indices = np.arange(PW, dtype=np.int64)
    phases = (indices[:, None] * indices[None, :] % PW).astype(np.float64) * (2.0 * math.pi / PW)
    factor = 1.0 / math.sqrt(PW)
    re = (np.cos(phases) * factor).astype(ml_dtypes.bfloat16)
    im = (-np.sin(phases) * factor).astype(ml_dtypes.bfloat16)
    forward = np.block([[re, im], [-im, re]])
    inverse = np.block([[re, -im], [im, re]])
    return forward.astype(ml_dtypes.bfloat16), inverse.astype(ml_dtypes.bfloat16)


class Here:
    def __init__(self):
        s = lax.axis_index("slab")
        a = lax.axis_index("angle")
        self.a = a
        self.c = lax.rem(s, 2)
        self.xl = lax.rem(lax.div(s, 2), 2)
        self.zc = lax.div(s, 4)
        self.y = lax.rem(a, NY)
        self.xh = lax.div(a, NY)
        self.m = self.xl * NZC + self.zc

    def z_of(self, rel):
        return lax.rem(self.zc + rel, NZC)

    def y_of(self, rel):
        return lax.rem(self.y + rel, NY)

    def x_of(self, flip):
        return 1 - self.xl if flip else self.xl

    def chip(self, rel_z, flip_x):
        return self.device(zc=self.z_of(rel_z), xl=self.x_of(flip_x))

    def angle_peer(self, flip_xh, rel_y):
        return self.device(xh=1 - self.xh if flip_xh else self.xh, y=self.y_of(rel_y))

    def device(self, zc=None, xl=None, c=None, xh=None, y=None):
        zc = self.zc if zc is None else zc
        xl = self.xl if xl is None else xl
        c = self.c if c is None else c
        xh = self.xh if xh is None else xh
        y = self.y if y is None else y
        return {"slab": zc * 4 + xl * 2 + c, "angle": xh * NY + y}

    @property
    def sibling(self):
        return self.device(c=1 - self.c)

    def greet(self):
        peers = [self.chip(r, f) for r in FAR_FIRST for f in (1, 0) if r or f]
        peers[8:8] = [self.angle_peer(f, r) for f in (1, 0) for r in (2, 1, 3, 0) if r or f]
        peers.append(self.sibling)
        barrier = pltpu.get_barrier_semaphore()
        for peer in peers:
            pl.semaphore_signal(barrier, 1, device_id=peer, device_id_type=pl.DeviceIdType.MESH)
        pl.semaphore_wait(barrier, len(peers))


def rows16(block):
    return pl.ds(pl.multiple_of(block * BLOCK, BLOCK), BLOCK)


def half_cols(core):
    return pl.ds(pl.multiple_of(core * HALF, HALF), HALF)


def chunk_cols(y):
    return pl.ds(pl.multiple_of(y * CHUNK, CHUNK), CHUNK)


def remote(src, dst, send, recv, to):
    return pltpu.make_async_remote_copy(
        src_ref=src,
        dst_ref=dst,
        send_sem=send,
        recv_sem=recv,
        device_id=to,
        device_id_type=pl.DeviceIdType.MESH,
    )


def shifted_tiles(tiles, start, count):
    first = start >> 7
    inner = start & (LANES - 1)
    need = min(count + 1, TILES)
    for level in (3, 2, 1, 0):
        stride = 1 << level
        keep = min(need + stride - 1, TILES)
        bit = (first >> level) & 1 == 1
        size = len(tiles)
        tiles = [lax.select_n(bit, tiles[j], tiles[(j + stride) % size]) for j in range(keep)]
    back = (LANES - inner) & (LANES - 1)
    lane = lax.broadcasted_iota(jnp.int32, tiles[0].shape, 1)
    stay = lane < LANES - inner
    turned = [pltpu.roll(tile.astype(jnp.float32), back, 1) for tile in tiles]
    return [jnp.where(stay, turned[j], turned[(j + 1) % need]) for j in range(count)]


def tiles_of(row):
    return [row[:, j * LANES : (j + 1) * LANES] for j in range(TILES)]


class Copies:
    def __init__(self, here):
        self.here = here
        self.sent = []

    def start(self, src, dst, send, recv, to):
        copy = remote(src, dst, send, recv, to)
        copy.start()
        self.sent.append(copy)

    def arrived(self, ref, recv):
        remote(ref, ref, recv, recv, self.here.sibling).wait_recv()

    def drain(self):
        for copy in self.sent:
            copy.wait_send()


WHOLE = ((1, 0), (0, 7), (0, 1), (1, 7), (1, 1))
PIECES = ((2, (0, 1)), (6, (0, 1)), (3, (0, 1)), (5, (0, 1)), (4, (0, 1)))
FWD = (0,)


def to_y(here, copies, piece, k, sems):
    send, recv = sems
    mine = piece(here.y)
    for d in (2, 1, 3):
        copies.start(mine, mine, send.at[d, k], recv.at[NY - d, k], here.angle_peer(0, d))


def from_y(here, copies, piece, k, sems):
    send, recv = sems
    for d in (1, 3, 2):
        copies.arrived(piece(here.y_of(d)), recv.at[d, k])


def project_kernel(
    vol, off, proj, offs_out, gath, acc, sib, offt, offv, off_s, offs_s,
    s_off, r_off, s_t1, r_t1, s_y, r_y, s_sib, r_sib, s_z, r_z, s_x, r_x, s_c, r_c, s_oa, r_oa, l_sem,
):
    here = Here()
    fetch = pltpu.make_async_copy(off, off_s, l_sem.at[2])
    fetch.start()
    here.greet()
    copies = Copies(here)
    order = (0, 1, 7, 2, 6, 3, 5, 4)
    cols = chunk_cols(here.y)

    def send_block(f, rel, where):
        r = (NZC - rel) % NZC
        to = here.chip(r, f)
        block = here.x_of(f) * NZC + here.z_of(r)
        copies.start(vol.at[rows16(block), where], gath.at[f, rel, :, where], s_t1.at[f, rel], r_t1.at[f, rel], to)

    for rel, flips in PIECES:
        for f in flips:
            send_block(f, rel, cols)
    for f, rel in WHOLE:
        send_block(f, rel, slice(None))
    own = pltpu.make_async_copy(vol.at[rows16(here.m)], gath.at[0, 0], l_sem.at[0])
    own.start()
    fetch.wait()
    offt[here.m] = jnp.full((1, LANES), off_s[0, 0], jnp.int32)
    for rel in order:
        for f in (0, 1):
            if rel or f:
                to = here.chip((NZC - rel) % NZC, f)
                copies.start(offt.at[here.m], offt.at[here.m], s_off.at[f, rel], r_off.at[f, rel], to)

    def piece(rel, flips):
        f = slice(None) if len(flips) == 2 else flips[0]
        return lambda y: gath.at[f, rel, :, chunk_cols(y)]

    for rel, flips in PIECES:
        for f in flips:
            copies.arrived(gath.at[f, rel, :, cols], r_t1.at[f, rel])
        to_y(here, copies, piece(rel, flips), rel, (s_y, r_y))

    for f in (0, 1):
        for r in range(NZC):
            if r or f:
                copies.arrived(offt.at[here.x_of(f) * NZC + here.z_of(r)], r_off.at[f, r])
    lane = lax.broadcasted_iota(jnp.int32, (1, LANES), 1)
    packed = jnp.zeros((1, LANES), jnp.int32)
    for g in range(NXL * NZC):
        packed = jnp.where(lane == g, offt[g], packed)
    offv[...] = packed
    down = pltpu.make_async_copy(offv, offs_s, l_sem.at[1])
    down.start()
    for f in (0, 1):
        for r in range(NY):
            if r or f:
                back = (NY - r) % NY
                copies.start(offv, offs_out.at[here.a], s_oa.at[f, r], r_oa.at[f, back], here.angle_peer(f, r))
    offs_out[here.a] = packed
    down.wait()
    own.wait()
    acc[...] = jnp.zeros_like(acc)

    def add_slot(f, rel):
        g = lax.rem(here.xl + f, NXL) * NZC + here.z_of(rel)
        for j, tile in enumerate(shifted_tiles(tiles_of(gath[f, rel]), offs_s[0, g], TILES)):
            acc[:, j * LANES : (j + 1) * LANES] += tile

    add_slot(0, 0)
    for f, rel in WHOLE:
        copies.arrived(gath.at[f, rel], r_t1.at[f, rel])
        add_slot(f, rel)
    for rel, flips in PIECES:
        from_y(here, copies, piece(rel, flips), rel, (s_y, r_y))
        for f in flips:
            add_slot(f, rel)

    mine, other = half_cols(here.c), half_cols(1 - here.c)
    copies.start(acc.at[:, other], sib, s_sib, r_sib, here.sibling)
    copies.arrived(sib, r_sib)
    proj[rows16(here.m), mine] = (acc[:, mine] + sib[...]).astype(jnp.bfloat16)

    own = proj.at[rows16(here.m), mine]
    for r in (1, 7, 2, 6, 3, 5, 4):
        copies.start(own, own, s_z.at[r], r_z.at[(NZC - r) % NZC], here.chip(r, 0))
    copies.start(own, own, s_x.at[0], r_x.at[0], here.chip(0, 1))
    copies.start(own, own, s_c.at[0, 0], r_c.at[0, 0], here.sibling)

    def along(rel):
        return proj.at[rows16(here.xl * NZC + here.z_of(rel)), mine]

    def across(rel):
        return proj.at[rows16(here.x_of(1) * NZC + here.z_of(rel)), mine]

    def take(f, rel, got, recv):
        copies.arrived(got, recv.at[rel])
        copies.start(got, got, s_c.at[f, rel], r_c.at[f, rel], here.sibling)

    for rel in (1, 7):
        take(0, rel, along(rel), r_z)
    take(1, 0, across(0), r_x)
    for r in (1, 7):
        copies.start(across(0), across(0), s_x.at[r], r_x.at[NZC - r], here.chip(r, 0))
    for rel in (2, 6, 3, 5, 4):
        copies.arrived(along(rel), r_z.at[rel])
        copies.start(along(rel), along(rel), s_x.at[rel], r_x.at[rel], here.chip(0, 1))
        copies.start(along(rel), along(rel), s_c.at[0, rel], r_c.at[0, rel], here.sibling)
    for rel in (1, 7, 2, 6, 3, 5, 4):
        take(1, rel, across(rel), r_x)
    for f in (0, 1):
        for rel in order:
            copies.arrived(proj.at[rows16(here.x_of(f) * NZC + here.z_of(rel)), other], r_c.at[f, rel])
    for f in (0, 1):
        for r in range(NY):
            if r or f:
                a_from = (1 - here.xh if f else here.xh) * NY + here.y_of(r)
                copies.arrived(offs_out.at[a_from], r_oa.at[f, r])
    copies.drain()


GROUP = 16
BATCHES = 2
LINES = BLOCK // BATCHES
PACK = HALF // 2
QUARTER = CHUNK // 2


def pack(x):
    n = x.shape[1] // 2
    return jnp.concatenate([x[:, :n], x[:, n:]], axis=0)


def unpack(x):
    return jnp.concatenate([x[:LINES], x[LINES:]], axis=1)


def wave_kernel(proj, probe, measured, pos, forward, inverse, out, total):
    total[...] = jnp.zeros_like(total)
    count = measured.shape[1] // PW

    def swap(x):
        n = x.shape[0] // PW
        parts = [[x[k * PW : (k + 1) * PW, h * PW : (h + 1) * PW] for k in range(n)] for h in range(2)]
        return jnp.concatenate([jnp.concatenate(p, axis=1) for p in parts], axis=0)

    def one_group(group, carry):
        p_re = probe[0].astype(jnp.float32)
        p_im = probe[1].astype(jnp.float32)
        fwd = forward[...]
        inv = inverse[...]
        starts = []
        exits = []
        for k in range(GROUP):
            at = pos[GROUP * group + k]
            first = jnp.minimum(lax.div(at, LANES), TILES - 2)
            inner = at - first * LANES
            where = pl.ds(pl.multiple_of(first * LANES, LANES), 2 * LANES)
            starts.append((where, inner))
            row = lax.broadcasted_iota(jnp.int32, (2 * LANES, PW), 0)
            col = lax.broadcasted_iota(jnp.int32, (2 * LANES, PW), 1)
            pick = jnp.where(row == col + inner, 1.0, 0.0).astype(jnp.bfloat16)
            patch = jnp.dot(proj[:, where], pick, preferred_element_type=jnp.float32)
            re, im = patch[:PW], patch[PW:]
            exits.append(
                jnp.concatenate([p_re * re - p_im * im, p_re * im + p_im * re], axis=1).astype(jnp.bfloat16)
            )
        half = jnp.dot(jnp.concatenate(exits, axis=0), fwd, preferred_element_type=jnp.float32).astype(jnp.bfloat16)
        far = jnp.dot(inv, swap(half), preferred_element_type=jnp.float32)
        waves = []
        for k in range(GROUP):
            f_re = far[:PW, k * PW : (k + 1) * PW]
            f_im = far[PW:, k * PW : (k + 1) * PW]
            at = pl.multiple_of((GROUP * group + k) * PW, PW)
            target = measured[:, pl.ds(at, PW)].astype(jnp.float32)
            misfit = f_re * f_re + f_im * f_im - target
            waves.append(jnp.concatenate([misfit * f_re, misfit * f_im], axis=1).astype(jnp.bfloat16))
        back = jnp.dot(jnp.concatenate(waves, axis=0), inv, preferred_element_type=jnp.float32).astype(jnp.bfloat16)
        grad = jnp.dot(fwd, swap(back), preferred_element_type=jnp.float32)
        placed = []
        for k, (where, inner) in enumerate(starts):
            g_re = grad[:PW, k * PW : (k + 1) * PW]
            g_im = grad[PW:, k * PW : (k + 1) * PW]
            patch_grad = jnp.concatenate(
                [p_re * g_re + p_im * g_im, p_re * g_im - p_im * g_re], axis=0
            ).astype(jnp.bfloat16)
            row = lax.broadcasted_iota(jnp.int32, (PW, 2 * LANES), 0)
            col = lax.broadcasted_iota(jnp.int32, (PW, 2 * LANES), 1)
            put = jnp.where(col == row + inner, 1.0, 0.0).astype(jnp.bfloat16)
            placed.append(jnp.dot(patch_grad, put, preferred_element_type=jnp.float32))
        for (where, inner), value in zip(starts, placed):
            total[:, where] += value
        return carry

    lax.fori_loop(0, count // GROUP, one_group, 0)
    for m in range(NXL * NZC):
        for h in range(BATCHES):
            for c in range(2):
                x = total[m * BLOCK + h * LINES : m * BLOCK + (h + 1) * LINES, c * HALF : (c + 1) * HALF]
                out[h, c, m] = pack(x).astype(jnp.bfloat16)


def volume_kernel(
    part, offs, out, cbuf, xsend, xbuf, zsend, zbuf, dgall, vsend,
    s_c, r_c, s_x, r_x, s_z, r_z, s_a, r_a, s_s, r_s, s_v, r_v, s_y, r_y,
):
    here = Here()
    here.greet()
    copies = Copies(here)
    f32 = jnp.float32
    batches = range(BATCHES)

    def block(f, r):
        return here.x_of(f) * NZC + here.z_of(r)

    for h in batches:
        for f in (1, 0):
            for r in FAR_FIRST:
                copies.start(
                    part.at[h, 1 - here.c, block(f, r)], cbuf.at[h, f, r], s_c.at[h, f, r], r_c.at[h, f, r], here.sibling
                )
    for h in batches:
        for r in FAR_FIRST:
            copies.arrived(cbuf.at[h, 1, r], r_c.at[h, 1, r])
            value = part[h, here.c, block(1, r)].astype(f32) + cbuf[h, 1, r].astype(f32)
            xsend[h, r] = value.astype(jnp.bfloat16)
            copies.start(xsend.at[h, r], xbuf.at[h, r], s_x.at[h, r], r_x.at[h, r], here.chip(0, 1))
    totals = []
    for h in batches:
        for r in FAR_FIRST:
            copies.arrived(cbuf.at[h, 0, r], r_c.at[h, 0, r])
            value = part[h, here.c, block(0, r)].astype(f32) + cbuf[h, 0, r].astype(f32)
            copies.arrived(xbuf.at[h, r], r_x.at[h, r])
            value = value + xbuf[h, r].astype(f32)
            if r:
                zsend[h, r] = value.astype(jnp.bfloat16)
                slot = (NZC - r) % NZC
                copies.start(zsend.at[h, r], zbuf.at[h, slot], s_z.at[h, r], r_z.at[h, slot], here.chip(r, 0))
            else:
                totals.append(value)
    peers = [(0, 1), (0, 3), (1, 0), (0, 2), (1, 1), (1, 3), (1, 2)]
    for h in batches:
        total = totals[h]
        for r in (1, 7, 2, 6, 3, 5, 4):
            copies.arrived(zbuf.at[h, r], r_z.at[h, r])
            total = total + zbuf[h, r].astype(f32)
        dgall[h, here.a, here.c] = total.astype(jnp.bfloat16)
        own = dgall.at[h, here.a, here.c]
        for f, r in reversed(peers):
            copies.start(own, own, s_a.at[h, f, r], r_a.at[h, f, (NY - r) % NY], here.angle_peer(f, r))
        copies.start(own, own, s_s.at[h, 0, 0], r_s.at[h, 0, 0], here.sibling)

    def angle_of(f, r):
        return (1 - here.xh if f else here.xh) * NY + here.y_of(r)

    def gradient(h, f, rel, start, count):
        g = here.x_of(f) * NZC + here.z_of((NZC - rel) % NZC)
        sums = None
        for b in range(ANGLES):
            first = (start + NX - offs[b, g]) & (NX - 1)
            tiles = []
            for c in range(2):
                row = unpack(dgall[h, b, c].astype(f32))
                tiles += [row[:, j * LANES : (j + 1) * LANES] for j in range(TILES // 2)]
            tiles = shifted_tiles(tiles, first, count)
            sums = tiles if sums is None else [x + t for x, t in zip(sums, tiles)]
        return sums

    def quarter(sums):
        return pack(jnp.concatenate(sums, axis=1)).astype(jnp.bfloat16)

    per = CHUNK // LANES

    def send_block(h, f, rel, src, dst):
        copies.start(src, dst, s_v.at[h, f, rel], r_v.at[h, f, rel], here.chip((NZC - rel) % NZC, f))

    for h in batches:
        for f, r in peers:
            got = dgall.at[h, angle_of(f, r), here.c]
            copies.arrived(got, r_a.at[h, f, r])
            copies.start(got, got, s_s.at[h, f, r], r_s.at[h, f, r], here.sibling)
        for f, r in [(0, 0)] + peers:
            copies.arrived(dgall.at[h, angle_of(f, r), 1 - here.c], r_s.at[h, f, r])
        for rel, flips in PIECES:
            for f in flips:
                vsend[h, f, rel, here.y] = quarter(gradient(h, f, rel, here.y * CHUNK, per))
                send_block(h, f, rel, vsend.at[h, f, rel, here.y], out.at[here.xl, here.zc, h, here.y])
        for f, rel in WHOLE:
            sums = gradient(h, f, rel, 0, TILES)
            for y in range(NY):
                vsend[h, f, rel, y] = quarter(sums[y * per : (y + 1) * per])
            send_block(h, f, rel, vsend.at[h, f, rel], out.at[here.xl, here.zc, h])
        sums = gradient(h, 0, 0, 0, TILES)
        for y in range(NY):
            out[here.xl, here.zc, h, y] = quarter(sums[y * per : (y + 1) * per])

    def piece(h, rel, flips):
        f = slice(None) if len(flips) == 2 else here.x_of(flips[0])
        return lambda y: out.at[f, here.z_of(rel), h, y]

    up, dn = here.angle_peer(0, 1), here.angle_peer(0, NY - 1)
    for h in batches:
        for rel, flips in PIECES:
            for f in flips:
                copies.arrived(out.at[here.x_of(f), here.z_of(rel), h, here.y], r_v.at[h, f, rel])
            mine = piece(h, rel, flips)(here.y)
            for d in (1, 3) if h in FWD else (2, 1, 3):
                copies.start(mine, mine, s_y.at[h, d, rel], r_y.at[h, NY - d, rel], here.angle_peer(0, d))
    for h in FWD:
        for k, (rel, flips) in enumerate(PIECES):
            d, to = ((3, up), (1, dn))[k % 2]
            got = piece(h, rel, flips)(here.y_of(d))
            copies.arrived(got, r_y.at[h, d, rel])
            copies.start(got, got, s_y.at[h, 2, rel], r_y.at[h, 2, rel], to)
    for h in batches:
        for f, rel in WHOLE:
            copies.arrived(out.at[here.x_of(f), here.z_of(rel), h], r_v.at[h, f, rel])
        for k, (rel, flips) in enumerate(PIECES):
            for d in (((1, 2), (3, 2))[k % 2]) if h in FWD else (1, 3, 2):
                copies.arrived(piece(h, rel, flips)(here.y_of(d)), r_y.at[h, d, rel])
    copies.drain()


def update_kernel(rate, grad, volume, consensus, out, made, sems):
    copies = []
    for m in range(NXL * NZC):
        rows = slice(m * BLOCK, (m + 1) * BLOCK)
        current = volume[rows].astype(jnp.float32)
        kept = current - MIX * (current - consensus[rows].astype(jnp.float32))
        for h in range(BATCHES):
            for y in range(NY):
                step = unpack(grad[m, h, y].astype(jnp.float32))
                lines = slice(h * LINES, (h + 1) * LINES)
                cols = slice(y * CHUNK, (y + 1) * CHUNK)
                made[m * BLOCK + h * LINES : m * BLOCK + (h + 1) * LINES, cols] = kept[lines, cols] - rate * step
        copies.append(pltpu.make_async_copy(made.at[rows], out.at[rows], sems.at[m]))
        copies[-1].start()
    for copy in copies:
        copy.wait()


def dma(*shape):
    return pltpu.SemaphoreType.DMA(shape)


def vmem():
    return pl.BlockSpec(memory_space=pltpu.VMEM)


def smem():
    return pl.BlockSpec(memory_space=pltpu.SMEM)


def project(lines, off):
    return pl.pallas_call(
        project_kernel,
        out_shape=(
            jax.ShapeDtypeStruct((2 * PW, NX), jnp.bfloat16),
            jax.ShapeDtypeStruct((ANGLES, 1, LANES), jnp.int32),
        ),
        in_specs=[pl.BlockSpec(memory_space=pl.ANY), pl.BlockSpec(memory_space=pl.ANY)],
        out_specs=(vmem(), vmem()),
        scratch_shapes=[
            pltpu.VMEM((NXL, NZC, BLOCK, NX), jnp.bfloat16),
            pltpu.VMEM((BLOCK, NX), jnp.float32),
            pltpu.VMEM((BLOCK, HALF), jnp.float32),
            pltpu.VMEM((NXL * NZC, 1, LANES), jnp.int32),
            pltpu.VMEM((1, LANES), jnp.int32),
            pltpu.SMEM((1, 1), jnp.int32),
            pltpu.SMEM((1, LANES), jnp.int32),
            dma(NXL, NZC), dma(NXL, NZC), dma(NXL, NZC), dma(NXL, NZC),
            dma(NY, NZC), dma(NY, NZC),
            pltpu.SemaphoreType.DMA, pltpu.SemaphoreType.DMA,
            dma(NZC), dma(NZC), dma(NZC), dma(NZC),
            dma(NXL, NZC), dma(NXL, NZC),
            dma(NXH, NY), dma(NXH, NY),
            dma(3),
        ],
        compiler_params=pltpu.CompilerParams(collective_id=0, has_side_effects=True, vmem_limit_bytes=52 * 1024 * 1024),
        name="project",
    )(lines, off)


def waves(proj, probe, measured, pos, forward, inverse):
    return pl.pallas_call(
        wave_kernel,
        out_shape=jax.ShapeDtypeStruct((BATCHES, 2, NXL * NZC, BLOCK, PACK), jnp.bfloat16),
        in_specs=[vmem(), vmem(), vmem(), smem(), vmem(), vmem()],
        out_specs=vmem(),
        scratch_shapes=[pltpu.VMEM((2 * PW, NX), jnp.float32)],
        compiler_params=pltpu.CompilerParams(vmem_limit_bytes=2 * VMEM),
        name="waves",
    )(proj, probe, measured, pos, forward, inverse)


def volume_gradient(part, offs):
    bf16 = jnp.bfloat16
    small = (BATCHES, NZC, BLOCK, PACK)
    return pl.pallas_call(
        volume_kernel,
        out_shape=jax.ShapeDtypeStruct((NXL, NZC, BATCHES, NY, BLOCK, QUARTER), bf16),
        in_specs=[vmem(), smem()],
        out_specs=vmem(),
        scratch_shapes=[
            pltpu.VMEM((BATCHES, NXL, NZC, BLOCK, PACK), bf16),
            pltpu.VMEM(small, bf16),
            pltpu.VMEM(small, bf16),
            pltpu.VMEM(small, bf16),
            pltpu.VMEM(small, bf16),
            pltpu.VMEM((BATCHES, ANGLES, 2, BLOCK, PACK), bf16),
            pltpu.VMEM((BATCHES, NXL, NZC, NY, BLOCK, QUARTER), bf16),
            dma(BATCHES, NXL, NZC), dma(BATCHES, NXL, NZC),
            dma(BATCHES, NZC), dma(BATCHES, NZC), dma(BATCHES, NZC), dma(BATCHES, NZC),
            dma(BATCHES, NXH, NY), dma(BATCHES, NXH, NY), dma(BATCHES, NXH, NY), dma(BATCHES, NXH, NY),
            dma(BATCHES, NXL, NZC), dma(BATCHES, NXL, NZC),
            dma(BATCHES, NY, NZC), dma(BATCHES, NY, NZC),
        ],
        compiler_params=pltpu.CompilerParams(collective_id=1, has_side_effects=True, vmem_limit_bytes=VMEM),
        cost_estimate=pl.CostEstimate(flops=10**8, bytes_accessed=10**8, transcendentals=0),
        name="volume_gradient",
    )(part, offs)


def update(rate, grad, lines, consensus):
    return pl.pallas_call(
        functools.partial(update_kernel, rate),
        out_shape=jax.ShapeDtypeStruct((2 * PW, NX), jnp.float32),
        in_specs=[vmem(), vmem(), vmem()],
        out_specs=pl.BlockSpec(memory_space=pl.ANY),
        scratch_shapes=[pltpu.VMEM((2 * PW, NX), jnp.float32), dma(NXL * NZC)],
        compiler_params=pltpu.CompilerParams(vmem_limit_bytes=VMEM),
        name="update",
    )(grad, lines, consensus)


def per_device(volume, consensus, probe, intensities, positions, offsets):
    pos_count = positions.shape[1]
    forward, inverse = dft_tables()
    lines = volume.reshape(2 * PW, NX)
    measured = intensities.reshape(PW, pos_count * PW)
    proj, offs = project(lines, offsets)
    part = waves(proj, probe, measured, positions.reshape(-1), jnp.asarray(forward), jnp.asarray(inverse))
    grad = volume_gradient(part, offs.reshape(ANGLES, LANES))
    rate = math.sqrt(NX / (pos_count * lax.axis_size("slab") * ANGLES * PW))
    grad = grad.reshape(NXL * NZC, BATCHES, NY, BLOCK, QUARTER)
    return update(rate, grad, lines, consensus.reshape(2 * PW, NX)).reshape(volume.shape)


def solution(mesh):
    return jax.shard_map(
        per_device,
        mesh=mesh,
        in_specs=(
            P(None, "slab", None, None),
            P(None, "slab", None, None),
            P(),
            P("angle", None, "slab", None),
            P("angle", "slab"),
            P("angle", "slab"),
        ),
        out_specs=P(None, "slab", None, None),
        check_vma=False,
    )
```
